512 devices in a mesh: patch: 64 (over x, z_lo, core), head: 8 (over y, z_hi).
Axes of the slice: x: 4, y: 4, z: 16 (z_hi: 2, z_lo: 8; z = z_hi * 8 + z_lo), core: 2. Of those that a mesh axis runs over, the one named last changes fastest.
Arguments:
- queries: bfloat16 [3072, 3072], P('patch', 'head'), as said below
- stale_kv: bfloat16 [2, 3072, 3072], P(None, None, 'head'), may hold values from -6 to 6, as said below
- codes: int32 [2, 3072, 3072], P(None, 'patch', 'head'), may hold values from -127 to 127
- exponents: int32 [2, 3072, 24], P(None, 'patch', 'head'), may hold values from -9 to -6
- text_kv: bfloat16 [2, 512, 3072], P(None, None, 'head'), may hold values from -6 to 6, as said below
- out_weight: bfloat16 [3072, 3072], P('head', 'patch'), may hold values from -0.109375 to 0.109375
- out_bias: float32 [3072], P('head'), may hold values from -0.6 to 0.6
- out_gate: float32 [3072], P('head'), may hold values from 2 to 8
Outputs:
- gated_out: bfloat16 [3072, 3072], P('patch', 'head')
The draws below stay inside these ranges and needn't reach their ends.
Inputs may be any that keep to these rules, and one draw needn't show every extreme that they name: queries are real-valued. `stale_kv`: last step's keys and values are real-valued. `text_kv`: text keys and values are real-valued.
All inputs are finite; a program needn't handle non-finite values.
Results may differ from the reference program's by a relative error of at most 0.0075.
Values may be sent and summed in bfloat16 or wider, within the bound.
A program may use at most 64 MiB of HBM per device.

```python
import math
import jax
import jax.numpy as jnp
from jax import lax

D = 3072
HEADS = 24
HD = 128
TEXT = 512
TOKENS = 3072


def draw_queries(key, part):
    key = jax.random.fold_in(key, 12)
    return (2.0 * jnp.clip(jax.random.normal(key, (TOKENS, HEADS * HD), jnp.float32), -4.0, 4.0)).astype(jnp.bfloat16)


def draw_stale_kv(key, part):
    key = jax.random.fold_in(key, 13)
    return jnp.clip(jax.random.normal(key, (2, TOKENS, HEADS * HD), jnp.float32), -6.0, 6.0).astype(jnp.bfloat16)


def draw_text_kv(key, part):
    key = jax.random.fold_in(key, 11)
    return jnp.clip(jax.random.normal(key, (2, TEXT, HEADS * HD), jnp.float32), -6.0, 6.0).astype(jnp.bfloat16)


def plant(values, own_key, smallest, largest):
    spot = [jax.random.randint(jax.random.fold_in(own_key, axis), (), 0, length) for axis, length in enumerate(values.shape)]
    longest = values.shape.index(max(values.shape))
    beside = spot[:longest] + [(spot[longest] + 1) % values.shape[longest]] + spot[longest + 1:]
    return values.at[tuple(spot)].set(smallest).at[tuple(beside)].set(largest)


def level_of(rng, shape, pieces, low, high):
    gain, own = 1.0, jax.random.fold_in(rng, 6)
    for dim, shards_of in pieces:
        steps = jnp.exp(jax.random.uniform(jax.random.fold_in(own, dim), (shards_of,), jnp.float32, low / len(pieces), high / len(pieces)))
        gain = gain * jnp.repeat(steps, shape[dim] // shards_of).reshape([-1 if axis == dim else 1 for axis in range(len(shape))])
    return gain


def centred(own_key, dims, width, reach, cuts=(), kind=jnp.bfloat16):
    gain = level_of(own_key, dims, cuts, -0.22, 0.18) if cuts else 1.0
    values = jax.random.normal(own_key, dims, jnp.float32) * width * gain
    return jnp.minimum(jnp.maximum(values, -reach), reach).astype(kind)


def setup_inputs(seed: int = 0) -> dict:
    streams_of = jax.random.split(jax.random.key(seed), 9)
    queries = draw_queries(jax.random.fold_in(streams_of[8], 71), 0)
    stale_kv = draw_stale_kv(jax.random.fold_in(streams_of[8], 71), 0)
    codes = plant(jax.random.randint(streams_of[2], (2, TOKENS, HEADS * HD), -127, 128), jax.random.fold_in(streams_of[2], 1), -127, 127).astype(jnp.int32)
    exponents = plant(jax.random.randint(streams_of[3], (2, TOKENS, HEADS), -9, -5), jax.random.fold_in(streams_of[3], 1), -9, (-5) - 1).astype(jnp.int32)
    text_kv = draw_text_kv(jax.random.fold_in(streams_of[8], 71), 0)
    out_weight = centred(streams_of[5], (HEADS * HD, D), (HEADS * HD) ** -0.5, 0.109375, ((0, 8), (1, 64)))
    out_bias = centred(streams_of[6], (D,), 0.1, 0.6, ((0, 8),), jnp.float32)
    out_gate = jnp.clip(jnp.exp(math.log(8.0) - 1.3862944 * jax.random.uniform(streams_of[7], (D,), jnp.float32) ** level_of(streams_of[7], (D,), ((0, 8),), -0.2, 0.2)), 2.0, 8.0)
    return {"queries": queries, "stale_kv": stale_kv, "codes": codes, "exponents": exponents, "text_kv": text_kv, "out_weight": out_weight, "out_bias": out_bias, "out_gate": out_gate}


def one_head(inputs):
    query, text_key, text_value, image_key, image_value = inputs
    text_scores = jnp.dot(query, text_key.T, preferred_element_type=jnp.float32)
    image_scores = jnp.dot(query.astype(jnp.float32), image_key.T, precision=lax.Precision.HIGHEST)
    scores = jnp.concatenate([text_scores, image_scores], axis=1) * (HD ** -0.5)
    row_peak = jnp.max(scores, axis=1, keepdims=True)
    weights = jnp.exp(scores - row_peak).astype(jnp.bfloat16)
    row_total = jnp.sum(weights.astype(jnp.float32), axis=1, keepdims=True)
    text_part = jnp.dot(weights[:, :TEXT], text_value, preferred_element_type=jnp.float32)
    image_part = jnp.dot(weights[:, TEXT:].astype(jnp.float32), image_value, precision=lax.Precision.HIGHEST)
    return ((text_part + image_part) / row_total).astype(jnp.bfloat16)


def reference(queries, stale_kv, codes, exponents, text_kv, out_weight, out_bias, out_gate):
    blocks = jnp.exp2(exponents.astype(jnp.float32))
    decoded = (codes.astype(jnp.float32).reshape(2, TOKENS, HEADS, HD) * blocks[..., None]).astype(jnp.bfloat16)
    rebuilt = stale_kv.astype(jnp.float32).reshape(2, TOKENS, HEADS, HD) + decoded.astype(jnp.float32)
    rebuilt = rebuilt.transpose(0, 2, 1, 3)
    query_heads = queries.reshape(TOKENS, HEADS, HD).transpose(1, 0, 2)
    text_heads = text_kv.reshape(2, TEXT, HEADS, HD).transpose(0, 2, 1, 3)
    attended = lax.map(one_head, (query_heads, text_heads[0], text_heads[1], rebuilt[0], rebuilt[1]))
    attended = attended.transpose(1, 0, 2).reshape(TOKENS, HEADS * HD)
    projected = jnp.dot(attended, out_weight, preferred_element_type=jnp.float32)
    return (out_gate * (projected + out_bias)).astype(jnp.bfloat16)
```

```python
import functools

import jax
import jax.numpy as jnp
from jax import lax
from jax.experimental import pallas as pl
from jax.experimental.pallas import tpu as pltpu
from jax.sharding import PartitionSpec as P

HD = 128
NX, NZ, NC, NY, NH = 4, 8, 2, 4, 2
BF = jnp.bfloat16
F32 = jnp.float32
NT = (((1,), (1,)), ((), ()))
NN = (((1,), (0,)), ((), ()))


def kernel(
    q_hbm, stale_hbm, codes_hbm, exps_hbm, text_hbm, w_hbm, bias_hbm, gate_hbm,
    out_ref,
    codes_v, exps_v, bias_v, gate_v, stale_v, text_v,
    q_all, kv, wt, o_send, o_recv, p_send, p_recv, z_send, z_recv,
    lsem, q_s, q_r, kv_s, kv_r, cf_s, cf_r, w1_s, w1_r, w2_s, w2_r, w3_s, w3_r,
    o_s, o_r, p_s, p_r, zz_s, zz_r,
):
    rows = q_hbm.shape[0]
    heads = q_hbm.shape[1] // HD
    width = q_hbm.shape[1]
    parts = NX * 2
    text_rows = text_hbm.shape[1] // parts
    p = lax.axis_index("patch")
    hd = lax.axis_index("head")
    x = lax.div(p, NZ * NC)
    z = lax.rem(lax.div(p, NC), NZ)
    c = lax.rem(p, NC)
    y = lax.div(hd, NH)
    zh = lax.rem(hd, NH)
    zi = lax.div(z, 2)
    par = lax.rem(z, 2)
    part = x * 2 + par

    def dev(xx=x, z_=z, cc=c, yy=y, hh=zh):
        return (xx * (NZ * NC) + z_ * NC + cc, yy * NH + hh)

    def up(v, k, n):
        return lax.rem(v + k, n)

    core_peer = dev(cc=1 - c)
    zh_peer = dev(hh=1 - zh)
    x_peers = [dev(xx=up(x, k, NX)) for k in (1, 2, 3)]
    y_peers = [dev(yy=up(y, k, NY)) for k in (1, 2, 3)]
    z_peers = [dev(z_=up(z, k, NZ)) for k in range(1, NZ)]
    zi_peers = [dev(z_=up(zi, k, 4) * 2 + par) for k in (1, 2, 3)]
    zx = zi * 2 + 1 - par
    pair_peers = [dev(xx=up(x, k, NX), z_=zx) for k in range(NX)]
    group = [(dev(xx=up(x, k, NX)), up(x, k, NX) * 2 + par, up(x, NX - k, NX) * 2 + par) for k in (1, 2, 3)]
    group += [(pair_peers[k], up(x, k, NX) * 2 + 1 - par, up(x, NX - k, NX) * 2 + 1 - par) for k in range(NX)]

    def remote(src, dst, s, r, to):
        return pltpu.make_async_remote_copy(
            src_ref=src, dst_ref=dst, send_sem=s, recv_sem=r, device_id=to, device_id_type=pl.DeviceIdType.MESH
        )

    barrier = pltpu.get_barrier_semaphore()
    everyone = [core_peer, zh_peer] + x_peers + y_peers + z_peers + pair_peers[1:]
    for peer in everyone:
        pl.semaphore_signal(barrier, inc=1, device_id=peer, device_id_type=pl.DeviceIdType.MESH)

    ld_codes = pltpu.make_async_copy(codes_hbm, codes_v, lsem.at[0])
    ld_exps = pltpu.make_async_copy(exps_hbm, exps_v, lsem.at[1])
    ld_w = pltpu.make_async_copy(w_hbm, wt.at[x, z, c], lsem.at[2])
    ld_q = pltpu.make_async_copy(q_hbm, q_all.at[part], lsem.at[3])
    ld_text = pltpu.make_async_copy(text_hbm.at[:, pl.ds(part * text_rows, text_rows)], text_v, lsem.at[4])
    ld_bias = pltpu.make_async_copy(bias_hbm, bias_v, lsem.at[5])
    ld_gate = pltpu.make_async_copy(gate_hbm, gate_v, lsem.at[6])
    ld_stale = [
        pltpu.make_async_copy(
            stale_hbm.at[:, pl.ds((x * (NZ * NC) + (2 * k + par) * NC) * rows, NC * rows)], stale_v.at[:, k], lsem.at[7 + k]
        )
        for k in range(4)
    ]
    loads = [ld_codes, ld_exps, ld_w, ld_q, ld_text, ld_bias, ld_gate] + ld_stale
    for ld in loads:
        ld.start()

    mine = zi * NC + c
    diagonal = lax.broadcasted_iota(jnp.int32, (rows, rows), 0) == lax.broadcasted_iota(jnp.int32, (rows, rows), 1)
    ones = jnp.ones((rows, HD), BF)
    ld_codes.wait()
    ld_exps.wait()
    for h in range(heads):
        code = codes_v[:, :, h * HD : (h + 1) * HD]
        for kind in range(2):
            step = jnp.left_shift(jnp.int32(1), exps_v[h, kind : kind + 1] + 9).astype(F32) * (2.0**-9)
            spread = jnp.where(diagonal, step, 0.0).astype(BF)
            step = lax.dot_general(spread, ones, NN, preferred_element_type=F32)
            kv[h, kind, mine] = (code[kind].astype(F32) * step).astype(BF)
    ld_w.wait()
    ld_q.wait()

    pl.semaphore_wait(barrier, len(everyone))

    pending = []

    def go(cp):
        cp.start()
        pending.append(cp)

    def send_kv(h):
        for k in (1, 2, 3):
            go(remote(kv.at[h, :, mine], kv.at[h, :, mine], kv_s.at[h, k - 1], kv_r.at[h, zi], zi_peers[k - 1]))

    send_kv(0)
    for k, (to, _, _) in enumerate(group):
        go(remote(q_all.at[part], q_all.at[part], q_s.at[k], q_r.at[part], to))
    go(remote(kv.at[:, :, mine], kv.at[:, :, mine], cf_s.at[0, 3], cf_r.at[0, 3], core_peer))
    for h in range(1, heads):
        send_kv(h)
    for k in range(1, NZ):
        go(remote(wt.at[x, z, c], wt.at[x, z, c], w1_s.at[k - 1], w1_r.at[z], z_peers[k - 1]))

    def pass_on(h):
        for k in (1, 2, 3):
            frm = up(zi, 4 - k, 4)
            slot = kv.at[h, :, frm * NC + c]
            remote(slot, slot, kv_s.at[h, k - 1], kv_r.at[h, frm], core_peer).wait_recv()
            go(remote(slot, slot, cf_s.at[h, k - 1], cf_r.at[h, k - 1], core_peer))

    def wait_core(h):
        for k in (1, 2, 3):
            slot = kv.at[h, :, up(zi, 4 - k, 4) * NC + 1 - c]
            remote(slot, slot, cf_s.at[h, k - 1], cf_r.at[h, k - 1], core_peer).wait_recv()

    scale = HD**-0.5
    tokens = parts * rows
    lane = lax.broadcasted_iota(jnp.int32, (tokens, HD), 1)
    stats = jnp.zeros((tokens, HD), F32)

    def attend(h, stats):
        cut = slice(h * HD, (h + 1) * HD)
        q = q_all[:, :, cut].reshape(tokens, HD)
        k_img = jnp.concatenate([stale_v[0, :, :, cut].reshape(tokens, HD), kv[h, 0].reshape(tokens, HD)], axis=1)
        v_img = jnp.concatenate([stale_v[1, :, :, cut].reshape(tokens, HD), kv[h, 1].reshape(tokens, HD)], axis=1)
        s_img = lax.dot_general(jnp.concatenate([q, q], axis=1), k_img, NT, preferred_element_type=F32)
        s_txt = lax.dot_general(q, text_v[0, :, cut], NT, preferred_element_type=F32)
        peak = jnp.maximum(jnp.max(s_img, axis=1, keepdims=True), jnp.max(s_txt, axis=1, keepdims=True))
        w_img = jnp.exp((s_img - peak) * scale).astype(BF)
        w_txt = jnp.exp((s_txt - peak) * scale).astype(BF)
        total = jnp.sum(w_img.astype(F32), axis=1, keepdims=True) + jnp.sum(w_txt.astype(F32), axis=1, keepdims=True)
        o_img = lax.dot_general(w_img, v_img, NN, preferred_element_type=F32)
        o_txt = lax.dot_general(w_txt, text_v[1, :, cut], NN, preferred_element_type=F32)
        o = (o_img[:, :HD] + o_img[:, HD:] + o_txt) / total
        o_send[:, h] = o.astype(BF).reshape(parts, rows, HD)
        stats = jnp.where(lax.div(lane, 3) == 2 * h, peak, stats)
        stats = jnp.where(lax.div(lane, 3) == 2 * h + 1, total, stats)
        return stats

    def send_o(h):
        span = pl.ds(h, 1 if h < heads - 1 else 2)
        for k, (to, slot, _) in enumerate(group):
            go(remote(o_send.at[slot, span], o_recv.at[part, span], o_s.at[h, k], o_r.at[h, part], to))

    pass_on(0)
    for k, (_, _, frm) in enumerate(group):
        remote(q_all.at[frm], q_all.at[frm], q_s.at[k], q_r.at[frm], core_peer).wait_recv()
    for ld in [ld_text, ld_bias, ld_gate] + ld_stale:
        ld.wait()
    other = kv.at[:, :, zi * NC + 1 - c]
    remote(other, other, cf_s.at[0, 3], cf_r.at[0, 3], core_peer).wait_recv()
    pass_on(1)
    wait_core(0)
    stats = attend(0, stats)
    send_o(0)
    pass_on(2)
    wait_core(1)
    stats = attend(1, stats)
    send_o(1)
    wait_core(2)
    stats = attend(2, stats)
    third = lax.rem(lane, 3)
    top = stats.astype(BF).astype(F32)
    mid = (stats - top).astype(BF).astype(F32)
    low = stats - top - mid
    o_send[:, heads] = jnp.where(third == 0, top, jnp.where(third == 1, mid, low)).astype(BF).reshape(parts, rows, HD)
    send_o(2)

    for k in range(1, NZ):
        frm = up(z, NZ - k, NZ)
        remote(wt.at[x, frm, c], wt.at[x, frm, c], w1_s.at[k - 1], w1_r.at[frm], core_peer).wait_recv()
    for k in (1, 2, 3):
        go(remote(wt.at[x, :, c], wt.at[x, :, c], w2_s.at[k - 1], w2_r.at[x], x_peers[k - 1]))

    o_recv[part] = o_send[part]
    for h in range(heads):
        span = pl.ds(h, 1 if h < heads - 1 else 2)
        for k, (_, _, frm) in enumerate(group):
            slot = o_recv.at[frm, span]
            remote(slot, slot, o_s.at[h, k], o_r.at[h, frm], core_peer).wait_recv()
    pick_row = lax.broadcasted_iota(jnp.int32, (HD, 2 * heads * HD), 0)
    pick_col = lax.broadcasted_iota(jnp.int32, (HD, 2 * heads * HD), 1)
    pick = (lax.div(pick_row, 3) == lax.div(pick_col, HD)).astype(F32).astype(BF)
    wide = lax.dot_general(o_recv[:, heads].reshape(tokens, HD), pick, NN, preferred_element_type=F32)
    wide = wide.reshape(parts, rows, 2 * heads * HD)
    cols = []
    for h in range(heads):
        peak = wide[:, :, 2 * h * HD : (2 * h + 1) * HD]
        total = wide[:, :, (2 * h + 1) * HD : (2 * h + 2) * HD]
        share = jnp.exp((peak - jnp.max(peak, axis=0, keepdims=True)) * scale) * total
        mix = jnp.sum(share * o_recv[:, h].astype(F32), axis=0) / jnp.sum(share, axis=0)
        cols.append(mix.astype(BF))
    attended = jnp.concatenate(cols, axis=1)

    for k in (1, 2, 3):
        frm = up(x, NX - k, NX)
        remote(wt.at[frm, :, c], wt.at[frm, :, c], w2_s.at[k - 1], w2_r.at[frm], core_peer).wait_recv()
    go(remote(wt.at[:, :, c], wt.at[:, :, c], w3_s, w3_r, core_peer))
    remote(wt.at[:, :, 1 - c], wt.at[:, :, 1 - c], w3_s, w3_r, core_peer).wait_recv()

    own = []
    for half in range(2):
        hh = (1 - zh) if half == 0 else zh
        for k in (1, 2, 3, 0):
            yy = up(y, k, NY)
            block = wt[yy, pl.ds(hh * 4, 4)].reshape(width, width)
            term = lax.dot_general(attended, block, NT, preferred_element_type=F32)
            if k:
                p_send[half, k - 1] = term.astype(BF)
                go(remote(p_send.at[half, k - 1], p_recv.at[half, y], p_s.at[half, k - 1], p_r.at[half, y], y_peers[k - 1]))
            else:
                own.append(term)

    def gather(half):
        acc = own[half]
        for k in (1, 2, 3):
            frm = up(y, NY - k, NY)
            slot = p_recv.at[half, frm]
            remote(slot, slot, p_s.at[half, k - 1], p_r.at[half, frm], core_peer).wait_recv()
            acc = acc + p_recv[half, frm].astype(F32)
        return acc

    z_send[...] = gather(0).astype(BF)
    go(remote(z_send, z_recv, zz_s, zz_r, zh_peer))
    near = gather(1) + bias_v[...].reshape(1, width)
    remote(z_send, z_recv, zz_s, zz_r, zh_peer).wait_recv()
    out_ref[...] = (gate_v[...].reshape(1, width) * (near + z_recv[...].astype(F32))).astype(BF)
    for cp in pending:
        cp.wait_send()


def body(queries, stale_kv, codes, exponents, text_kv, out_weight, out_bias, out_gate):
    rows, width = queries.shape
    heads = width // HD
    parts = NX * 2
    dma = pltpu.SemaphoreType.DMA
    any_spec = pl.BlockSpec(memory_space=pl.ANY)
    return pl.pallas_call(
        kernel,
        out_shape=jax.ShapeDtypeStruct((rows, width), BF),
        in_specs=[any_spec] * 8,
        out_specs=pl.BlockSpec(memory_space=pltpu.VMEM),
        scratch_shapes=[
            pltpu.VMEM(codes.shape, jnp.int32),
            pltpu.VMEM((heads, 2, rows), jnp.int32),
            pltpu.VMEM((width,), F32),
            pltpu.VMEM((width,), F32),
            pltpu.VMEM((2, 4, NC * rows, width), BF),
            pltpu.VMEM((2, text_kv.shape[1] // parts, width), BF),
            pltpu.VMEM((parts, rows, width), BF),
            pltpu.VMEM((heads, 2, 8, rows, HD), BF),
            pltpu.VMEM((NX, NZ, NC, rows, width), BF),
            pltpu.VMEM((parts, heads + 1, rows, HD), BF),
            pltpu.VMEM((parts, heads + 1, rows, HD), BF),
            pltpu.VMEM((2, 3, rows, width), BF),
            pltpu.VMEM((2, NY, rows, width), BF),
            pltpu.VMEM((rows, width), BF),
            pltpu.VMEM((rows, width), BF),
            dma((11,)),
            dma((7,)), dma((parts,)),
            dma((heads, 3)), dma((heads, 4)),
            dma((heads, 4)), dma((heads, 4)),
            dma((7,)), dma((NZ,)),
            dma((3,)), dma((NX,)),
            dma(()), dma(()),
            dma((heads, 7)), dma((heads, parts)),
            dma((2, 3)), dma((2, NY)),
            dma(()), dma(()),
        ],
        compiler_params=pltpu.CompilerParams(
            collective_id=0, has_side_effects=True, vmem_limit_bytes=60 * 1024 * 1024
        ),
        cost_estimate=pl.CostEstimate(flops=640_000_000, bytes_accessed=4_000_000, transcendentals=520_000),
        name="joint_attention",
    )(
        queries, stale_kv, codes, exponents.transpose(2, 0, 1), text_kv, out_weight.T,
        out_bias, out_gate,
    )


def solution(mesh):
    placed = (
        P("patch", "head"),
        P(None, None, "head"),
        P(None, "patch", "head"),
        P(None, "patch", "head"),
        P(None, None, "head"),
        P("head", "patch"),
        P("head"),
        P("head"),
    )
    return jax.shard_map(
        body, mesh=mesh, in_specs=placed, out_specs=P("patch", "head"), check_vma=False
    )
```

```python
import jax
import jax.numpy as jnp
from jax import lax
from jax.experimental import pallas as pl
from jax.experimental.pallas import tpu as pltpu
from jax.sharding import PartitionSpec as P

HD = 128
NX, NZ, NC, NY, NH = 4, 8, 2, 4, 2
QUAD = 4
BF = jnp.bfloat16
F32 = jnp.float32
MESH = pl.DeviceIdType.MESH
NT = (((1,), (1,)), ((), ()))
NN = (((1,), (0,)), ((), ()))


def kernel(
    q_hbm, stale_hbm, codes_hbm, exps_hbm, text_hbm, w_hbm, bias_hbm, gate_hbm,
    out_ref,
    codes_v, exps_v, bias_v, gate_v, stale_v, text_v,
    q_all, kv, wt, o_send, o_recv, p_send, p_recv, z_send, z_recv,
    lsem, q_s, q_r, kh_s, kh_r, kx_s, kx_r, kf_s, kf_r, kc_s, kc_r,
    wh_s, wh_r, wq_s, wq_r, wx_s, wx_r, wf_s, wf_r, wc_s, wc_r,
    o_s, o_r, p_s, p_r, zz_s, zz_r, entered,
):
    rows, width = q_hbm.shape
    heads = width // HD
    text_rows = text_hbm.shape[1] // QUAD
    p = lax.axis_index("patch")
    hd = lax.axis_index("head")
    x = lax.div(p, NZ * NC)
    z = lax.rem(lax.div(p, NC), NZ)
    c = lax.rem(p, NC)
    y = lax.div(hd, NH)
    zh = lax.rem(hd, NH)
    zb = lax.div(z, QUAD)
    zq = lax.rem(z, QUAD)

    def dev(xx=x, z_=z, cc=c, yy=y, hh=zh):
        return (xx * (NZ * NC) + z_ * NC + cc, yy * NH + hh)

    def ring(k):
        at = lax.rem(zh * NZ + z + k, NZ * NH)
        return dev(z_=lax.rem(at, NZ), hh=lax.div(at, NZ))

    core_peer = dev(cc=1 - c)
    half_peer = dev(z_=(1 - zb) * QUAD + zq)
    zh_peer = dev(hh=1 - zh)
    x_at = [lax.rem(x + k, NX) for k in (1, 2, 3)]
    y_at = [lax.rem(y + k, NY) for k in (1, 2, 3)]
    q_at = [lax.rem(zq + k, QUAD) for k in (1, 2, 3)]
    x_peers = [dev(xx=v) for v in x_at]
    y_peers = [dev(yy=v) for v in y_at]
    q_peers = [dev(z_=zb * QUAD + v) for v in q_at]

    pending = []

    def send(src, dst, s, r, to):
        cp = pltpu.make_async_remote_copy(
            src_ref=src, dst_ref=dst, send_sem=s, recv_sem=r, device_id=to, device_id_type=MESH
        )
        cp.start()
        pending.append(cp)

    def arrive(dst, s, r):
        pltpu.make_async_remote_copy(
            src_ref=dst, dst_ref=dst, send_sem=s, recv_sem=r, device_id=core_peer, device_id_type=MESH
        ).wait_recv()

    barrier = pltpu.get_barrier_semaphore()
    everyone = [ring(4), ring(NZ * NH - 4), core_peer] + x_peers + y_peers + q_peers
    for peer in everyone:
        pl.semaphore_signal(barrier, inc=1, device_id=peer, device_id_type=MESH)

    ld_codes = pltpu.make_async_copy(codes_hbm, codes_v, lsem.at[0])
    ld_exps = pltpu.make_async_copy(exps_hbm, exps_v, lsem.at[1])
    ld_w = pltpu.make_async_copy(w_hbm, wt.at[zb, x, 0, c], lsem.at[2])
    ld_q = pltpu.make_async_copy(q_hbm, q_all.at[zq], lsem.at[3])
    ld_text = pltpu.make_async_copy(text_hbm.at[:, pl.ds(zq * text_rows, text_rows)], text_v, lsem.at[4])
    ld_bias = pltpu.make_async_copy(bias_hbm, bias_v, lsem.at[5])
    ld_gate = pltpu.make_async_copy(gate_hbm, gate_v, lsem.at[6])
    ld_stale = [
        pltpu.make_async_copy(
            stale_hbm.at[:, pl.ds((xx * NZ + b * QUAD + zq) * NC * rows, NC * rows)],
            stale_v.at[:, xx, b], lsem.at[7 + xx * 2 + b],
        )
        for xx in range(NX) for b in range(2)
    ]
    for ld in [ld_codes, ld_exps, ld_w, ld_q, ld_text, ld_bias, ld_gate] + ld_stale:
        ld.start()

    diagonal = lax.broadcasted_iota(jnp.int32, (rows, rows), 0) == lax.broadcasted_iota(jnp.int32, (rows, rows), 1)
    ones = jnp.ones((rows, HD), BF)
    ld_codes.wait()
    ld_exps.wait()
    for h in range(heads):
        code = codes_v[:, :, h * HD : (h + 1) * HD]
        for kind in range(2):
            step = jnp.left_shift(jnp.int32(1), exps_v[h, kind : kind + 1] + 9).astype(F32) * (2.0**-9)
            spread = jnp.where(diagonal, step, 0.0).astype(BF)
            step = lax.dot_general(spread, ones, NN, preferred_element_type=F32)
            kv[h, kind, x, zb, c] = (code[kind].astype(F32) * step).astype(BF)
    ld_w.wait()
    ld_q.wait()

    pl.semaphore_wait(barrier, len(everyone))
    pl.semaphore_signal(entered, inc=1, device_id=ring(4), device_id_type=MESH)

    def send_half(h):
        mine = kv.at[h, :, x, zb, c]
        send(mine, mine, kh_s.at[h], kh_r.at[h], half_peer)

    send_half(0)
    for k in range(3):
        send(q_all.at[zq], q_all.at[zq], q_s.at[k], q_r.at[zq], q_peers[k])
    for h in range(1, heads):
        send_half(h)
    for k in range(3):
        mine = kv.at[:, :, x, zb, c]
        send(mine, mine, kx_s.at[k], kx_r.at[x], x_peers[k])
    own_w = wt.at[zb, x, 0, c]
    send(own_w, own_w, wh_s, wh_r, half_peer)
    for k in range(3):
        send(own_w, wt.at[zb, x, 3 - k, c], wq_s.at[0, k], wq_r.at[0, 3 - k], q_peers[k])
    for k in range(3):
        send(own_w, own_w, wx_s.at[0, k], wx_r.at[0, x], x_peers[k])

    def from_x(h):
        for k in range(3):
            slot = kv.at[h, :, x_at[k], 1 - zb, c]
            arrive(slot, kf_s.at[h, k], kf_r.at[h, x_at[k]])
        slot = kv.at[h, :, :, 1 - zb, c]
        send(slot, slot, kc_s.at[1 + h], kc_r.at[1 + h], core_peer)

    def from_core(h):
        slot = kv.at[h, :, :, 1 - zb, 1 - c]
        arrive(slot, kc_s.at[1 + h], kc_r.at[1 + h])

    scale = HD**-0.5
    tokens = QUAD * rows
    keys = NX * 2 * NC * rows
    lane = lax.broadcasted_iota(jnp.int32, (tokens, HD), 1)

    def attend(h, stats):
        cut = slice(h * HD, (h + 1) * HD)
        q = q_all[:, :, cut].reshape(tokens, HD)
        k_img = jnp.concatenate([stale_v[0, :, :, :, cut].reshape(keys, HD), kv[h, 0].reshape(keys, HD)], axis=1)
        v_img = jnp.concatenate([stale_v[1, :, :, :, cut].reshape(keys, HD), kv[h, 1].reshape(keys, HD)], axis=1)
        s_img = lax.dot_general(jnp.concatenate([q, q], axis=1), k_img, NT, preferred_element_type=F32)
        s_txt = lax.dot_general(q, text_v[0, :, cut], NT, preferred_element_type=F32)
        peak = jnp.maximum(jnp.max(s_img, axis=1, keepdims=True), jnp.max(s_txt, axis=1, keepdims=True))
        w_img = jnp.exp((s_img - peak) * scale).astype(BF)
        w_txt = jnp.exp((s_txt - peak) * scale).astype(BF)
        total = jnp.sum(w_img.astype(F32), axis=1, keepdims=True) + jnp.sum(w_txt.astype(F32), axis=1, keepdims=True)
        o_img = lax.dot_general(w_img, v_img, NN, preferred_element_type=F32)
        o_txt = lax.dot_general(w_txt, text_v[1, :, cut], NN, preferred_element_type=F32)
        o = (o_img[:, :HD] + o_img[:, HD:] + o_txt) / total
        o_send[:, h] = o.astype(BF).reshape(QUAD, rows, HD)
        stats = jnp.where(lax.div(lane, 3) == 2 * h, peak, stats)
        stats = jnp.where(lax.div(lane, 3) == 2 * h + 1, total, stats)
        return stats

    def send_o(h):
        span = pl.ds(h, 1 if h < heads - 1 else 2)
        for k in range(3):
            send(o_send.at[q_at[k], span], o_recv.at[zq, span], o_s.at[h, k], o_r.at[h, zq], q_peers[k])

    for h in range(heads):
        slot = kv.at[h, :, x, 1 - zb, c]
        arrive(slot, kh_s.at[h], kh_r.at[h])
        for k in range(3):
            send(slot, slot, kf_s.at[h, k], kf_r.at[h, x], x_peers[k])
        if h == 0:
            for k in range(3):
                there = kv.at[:, :, x_at[k], zb, c]
                arrive(there, kx_s.at[k], kx_r.at[x_at[k]])
            all_x = kv.at[:, :, :, zb, c]
            send(all_x, all_x, kc_s.at[0], kc_r.at[0], core_peer)
    half_w = wt.at[1 - zb, x, 0, c]
    arrive(half_w, wh_s, wh_r)
    for k in range(3):
        send(half_w, wt.at[1 - zb, x, 3 - k, c], wq_s.at[1, k], wq_r.at[1, 3 - k], q_peers[k])
    for k in range(3):
        send(half_w, half_w, wx_s.at[1, k], wx_r.at[1, x], x_peers[k])

    def spread_w(b, side):
        for k in range(3):
            arrive(wt.at[side, x, k + 1, c], wq_s.at[b, k], wq_r.at[b, k + 1])
        rest = wt.at[side, x, pl.ds(1, 3), c]
        for k in range(3):
            send(rest, rest, wf_s.at[b, k], wf_r.at[b, x], x_peers[k])

    def cross_w(b, side):
        for k in range(3):
            arrive(wt.at[side, x_at[k], 0, c], wx_s.at[b, k], wx_r.at[b, x_at[k]])
            arrive(wt.at[side, x_at[k], pl.ds(1, 3), c], wf_s.at[b, k], wf_r.at[b, x_at[k]])
        mine = wt.at[side, :, :, c]
        send(mine, mine, wc_s.at[b], wc_r.at[side], core_peer)

    for k in range(3):
        arrive(q_all.at[q_at[k]], q_s.at[k], q_r.at[q_at[k]])
    for ld in [ld_text, ld_bias, ld_gate] + ld_stale:
        ld.wait()
    from_x(0)
    spread_w(0, zb)
    from_x(1)
    all_x = kv.at[:, :, :, zb, 1 - c]
    arrive(all_x, kc_s.at[0], kc_r.at[0])
    from_core(0)
    stats = attend(0, jnp.zeros((tokens, HD), F32))
    send_o(0)
    from_x(2)
    from_core(1)
    stats = attend(1, stats)
    send_o(1)
    from_core(2)
    stats = attend(2, stats)
    third = lax.rem(lane, 3)
    top = stats.astype(BF).astype(F32)
    mid = (stats - top).astype(BF).astype(F32)
    low = stats - top - mid
    o_send[:, heads] = jnp.where(third == 0, top, jnp.where(third == 1, mid, low)).astype(BF).reshape(QUAD, rows, HD)
    send_o(2)
    spread_w(1, 1 - zb)
    cross_w(0, zb)

    o_recv[zq] = o_send[zq]

    def from_quad(h):
        span = pl.ds(h, 1 if h < heads - 1 else 2)
        for k in range(3):
            arrive(o_recv.at[q_at[k], span], o_s.at[h, k], o_r.at[h, q_at[k]])

    from_quad(0)
    from_quad(1)
    from_quad(2)
    pick_row = lax.broadcasted_iota(jnp.int32, (HD, 2 * heads * HD), 0)
    pick_col = lax.broadcasted_iota(jnp.int32, (HD, 2 * heads * HD), 1)
    pick = (lax.div(pick_row, 3) == lax.div(pick_col, HD)).astype(F32).astype(BF)
    wide = lax.dot_general(o_recv[:, heads].reshape(tokens, HD), pick, NN, preferred_element_type=F32)
    wide = wide.reshape(QUAD, rows, 2 * heads * HD)
    cols = []
    for h in range(heads):
        peak = wide[:, :, 2 * h * HD : (2 * h + 1) * HD]
        total = wide[:, :, (2 * h + 1) * HD : (2 * h + 2) * HD]
        share = jnp.exp((peak - jnp.max(peak, axis=0, keepdims=True)) * scale) * total
        mix = jnp.sum(share * o_recv[:, h].astype(F32), axis=0) / jnp.sum(share, axis=0)
        cols.append(mix.astype(BF))
    attended = jnp.concatenate(cols, axis=1)

    cross_w(1, 1 - zb)
    for b, side in ((0, zb), (1, 1 - zb)):
        arrive(wt.at[side, :, :, 1 - c], wc_s.at[b], wc_r.at[side])

    own = []
    for half in range(2):
        side = (1 - zh) if half == 0 else zh
        for k in (0, 1, 2, 3):
            to = y_at[k] if k < 3 else y
            pieces = [wt[side, to, lax.rem(v + QUAD - zq, QUAD)].reshape(NC * rows, width) for v in range(QUAD)]
            term = lax.dot_general(attended, jnp.concatenate(pieces, axis=0), NT, preferred_element_type=F32)
            if k < 3:
                p_send[half, k] = term.astype(BF)
                send(p_send.at[half, k], p_recv.at[half, y], p_s.at[half, k], p_r.at[half, y], y_peers[k])
            else:
                own.append(term)

    def gather(half):
        acc = own[half]
        for k in range(3):
            arrive(p_recv.at[half, y_at[k]], p_s.at[half, k], p_r.at[half, y_at[k]])
            acc = acc + p_recv[half, y_at[k]].astype(F32)
        return acc

    z_send[...] = gather(0).astype(BF)
    pl.semaphore_wait(entered, 1)
    send(z_send, z_recv, zz_s, zz_r, zh_peer)
    near = gather(1) + bias_v[...].reshape(1, width)
    arrive(z_recv, zz_s, zz_r)
    out_ref[...] = (gate_v[...].reshape(1, width) * (near + z_recv[...].astype(F32))).astype(BF)
    for cp in pending:
        cp.wait_send()


def body(queries, stale_kv, codes, exponents, text_kv, out_weight, out_bias, out_gate):
    rows, width = queries.shape
    heads = width // HD
    dma = pltpu.SemaphoreType.DMA
    any_spec = pl.BlockSpec(memory_space=pl.ANY)
    return pl.pallas_call(
        kernel,
        out_shape=jax.ShapeDtypeStruct((rows, width), BF),
        in_specs=[any_spec] * 8,
        out_specs=pl.BlockSpec(memory_space=pltpu.VMEM),
        scratch_shapes=[
            pltpu.VMEM(codes.shape, jnp.int32),
            pltpu.VMEM((heads, 2, rows), jnp.int32),
            pltpu.VMEM((width,), F32),
            pltpu.VMEM((width,), F32),
            pltpu.VMEM((2, NX, 2, NC * rows, width), BF),
            pltpu.VMEM((2, text_kv.shape[1] // QUAD, width), BF),
            pltpu.VMEM((QUAD, rows, width), BF),
            pltpu.VMEM((heads, 2, NX, 2, NC, rows, HD), BF),
            pltpu.VMEM((2, NX, QUAD, NC, rows, width), BF),
            pltpu.VMEM((QUAD, heads + 1, rows, HD), BF),
            pltpu.VMEM((QUAD, heads + 1, rows, HD), BF),
            pltpu.VMEM((2, 3, rows, width), BF),
            pltpu.VMEM((2, NY, rows, width), BF),
            pltpu.VMEM((rows, width), BF),
            pltpu.VMEM((rows, width), BF),
            dma((15,)),
            dma((3,)), dma((QUAD,)),
            dma((heads,)), dma((heads,)),
            dma((3,)), dma((NX,)),
            dma((heads, 3)), dma((heads, NX)),
            dma((heads + 1,)), dma((heads + 1,)),
            dma(()), dma(()),
            dma((2, 3)), dma((2, QUAD)),
            dma((2, 3)), dma((2, NX)),
            dma((2, 3)), dma((2, NX)),
            dma((2,)), dma((2,)),
            dma((heads, 3)), dma((heads, QUAD)),
            dma((2, 3)), dma((2, NY)),
            dma(()), dma(()),
            pltpu.SemaphoreType.REGULAR,
        ],
        compiler_params=pltpu.CompilerParams(
            collective_id=0, has_side_effects=True, vmem_limit_bytes=60 * 1024 * 1024
        ),
        cost_estimate=pl.CostEstimate(flops=640_000_000, bytes_accessed=4_000_000, transcendentals=520_000),
        name="joint_attention",
    )(
        queries, stale_kv, codes, exponents.transpose(2, 0, 1), text_kv, out_weight.T,
        out_bias, out_gate,
    )


def solution(mesh):
    placed = (
        P("patch", "head"),
        P(None, None, "head"),
        P(None, "patch", "head"),
        P(None, "patch", "head"),
        P(None, None, "head"),
        P("head", "patch"),
        P("head"),
        P("head"),
    )
    return jax.shard_map(
        body, mesh=mesh, in_specs=placed, out_specs=P("patch", "head"), check_vma=False
    )
```

```python
import jax
import jax.numpy as jnp
from jax import lax
from jax.experimental import pallas as pl
from jax.experimental.pallas import tpu as pltpu
from jax.sharding import PartitionSpec as P

HD = 128
NX, NZ, NC, NY, NH = 4, 8, 2, 4, 2
QUAD = 4
BF = jnp.bfloat16
F32 = jnp.float32
MESH = pl.DeviceIdType.MESH
NT = (((1,), (1,)), ((), ()))
NN = (((1,), (0,)), ((), ()))
TN = (((0,), (0,)), ((), ()))
STATS = 16


def kernel(
    q_hbm, stale_hbm, codes_hbm, exps_hbm, text_hbm, w_hbm, bias_hbm, gate_hbm,
    out_ref,
    codes_v, exps_v, bias_v, gate_v, stale_v, text_v,
    q_all, kv, wt, o_send, o_recv, a_all, p_send, p_recv, z_send, z_recv,
    lsem, q_s, q_r, kh_s, kh_r, kx_s, kx_r, kf_s, kf_r, kc_s, kc_r,
    wh_s, wh_r, wq_s, wq_r, wc_s, wc_r, o_s, o_r, a_s, a_r, p_s, p_r, zz_s, zz_r, entered,
):
    rows, width = q_hbm.shape
    heads = width // HD
    text_rows = text_hbm.shape[1] // QUAD
    p = lax.axis_index("patch")
    hd = lax.axis_index("head")
    x = lax.div(p, NZ * NC)
    z = lax.rem(lax.div(p, NC), NZ)
    c = lax.rem(p, NC)
    y = lax.div(hd, NH)
    zh = lax.rem(hd, NH)
    zb = lax.div(z, QUAD)
    zq = lax.rem(z, QUAD)
    far, near = 1 - zh, zh

    def dev(xx=x, z_=z, cc=c, yy=y, hh=zh):
        return (xx * (NZ * NC) + z_ * NC + cc, yy * NH + hh)

    def ring(k):
        at = lax.rem(zh * NZ + z + k, NZ * NH)
        return dev(z_=lax.rem(at, NZ), hh=lax.div(at, NZ))

    core_peer = dev(cc=1 - c)
    half_peer = dev(z_=(1 - zb) * QUAD + zq)
    zh_peer = dev(hh=1 - zh)
    x_at = [lax.rem(x + k, NX) for k in (1, 2, 3)]
    y_at = [lax.rem(y + k, NY) for k in (1, 2, 3)]
    q_at = [lax.rem(zq + k, QUAD) for k in (1, 2, 3)]
    x_peers = [dev(xx=v) for v in x_at]
    feature_peers = [dev(xx=v, yy=x) for v in x_at]
    feature_home = dev(yy=x)
    feature_from = [dev(xx=y, yy=v) for v in y_at]
    away = x != y
    feature_near = dev(xx=y, cc=jnp.where(away, c, 1 - c))
    q_peers = [dev(z_=zb * QUAD + v) for v in q_at]

    pending = []

    def send(src, dst, s, r, to):
        cp = pltpu.make_async_remote_copy(
            src_ref=src, dst_ref=dst, send_sem=s, recv_sem=r, device_id=to, device_id_type=MESH
        )
        cp.start()
        pending.append(cp)

    def arrive(dst, s, r):
        pltpu.make_async_remote_copy(
            src_ref=dst, dst_ref=dst, send_sem=s, recv_sem=r, device_id=core_peer, device_id_type=MESH
        ).wait_recv()

    barrier = pltpu.get_barrier_semaphore()
    everyone = [ring(4), ring(NZ * NH - 4), core_peer] + x_peers + q_peers
    for peer in everyone + feature_from + [feature_near]:
        pl.semaphore_signal(barrier, inc=1, device_id=peer, device_id_type=MESH)

    ld_codes = pltpu.make_async_copy(codes_hbm, codes_v, lsem.at[0])
    ld_exps = pltpu.make_async_copy(exps_hbm, exps_v, lsem.at[1])
    ld_w = pltpu.make_async_copy(w_hbm, wt.at[zb, 0, c], lsem.at[2])
    ld_q = pltpu.make_async_copy(q_hbm, q_all.at[zq], lsem.at[3])
    ld_text = pltpu.make_async_copy(text_hbm.at[:, pl.ds(zq * text_rows, text_rows)], text_v, lsem.at[4])
    ld_bias = pltpu.make_async_copy(bias_hbm, bias_v, lsem.at[5])
    ld_gate = pltpu.make_async_copy(gate_hbm, gate_v, lsem.at[6])
    ld_stale = [
        pltpu.make_async_copy(
            stale_hbm.at[:, pl.ds((xx * NZ + b * QUAD + zq) * NC * rows, NC * rows)],
            stale_v.at[:, xx, b], lsem.at[7 + xx * 2 + b],
        )
        for xx in range(NX) for b in range(2)
    ]
    for ld in [ld_codes, ld_exps, ld_w, ld_q, ld_text, ld_bias, ld_gate] + ld_stale:
        ld.start()

    diagonal = lax.broadcasted_iota(jnp.int32, (rows, rows), 0) == lax.broadcasted_iota(jnp.int32, (rows, rows), 1)
    ones = jnp.ones((rows, HD), BF)
    ld_codes.wait()
    ld_exps.wait()
    for h in range(heads):
        code = codes_v[:, :, h * HD : (h + 1) * HD]
        for kind in range(2):
            step = jnp.left_shift(jnp.int32(1), exps_v[h, kind : kind + 1] + 9).astype(F32) * (2.0**-9)
            spread = jnp.where(diagonal, step, 0.0).astype(BF)
            step = lax.dot_general(spread, ones, NN, preferred_element_type=F32)
            kv[h, kind, x, zb, c] = (code[kind].astype(F32) * step).astype(BF)
    ld_w.wait()
    ld_q.wait()

    pl.semaphore_wait(barrier, len(everyone) + 4)
    pl.semaphore_signal(entered, inc=1, device_id=ring(4), device_id_type=MESH)

    def kv_half(h):
        mine = kv.at[h, :, x, zb, c]
        send(mine, mine, kh_s.at[h], kh_r.at[h], half_peer)

    def kv_x():
        for k in range(3):
            mine = kv.at[:, :, x, zb, c]
            send(mine, mine, kx_s.at[k], kx_r.at[x], x_peers[k])

    def q_quad():
        for k in range(3):
            send(q_all.at[zq], q_all.at[zq], q_s.at[k], q_r.at[zq], q_peers[k])

    own_w = wt.at[zb, 0, c]
    half_w = wt.at[1 - zb, 0, c]

    def w_half():
        send(own_w, own_w, wh_s, wh_r, half_peer)

    def w_got_half():
        arrive(half_w, wh_s, wh_r)

    def w_quad(side):
        for k in range(3):
            send(wt.at[side, 0, c], wt.at[side, 3 - k, c], wq_s.at[side, k], wq_r.at[side, 3 - k], q_peers[k])

    def w_core(side):
        for k in range(3):
            arrive(wt.at[side, k + 1, c], wq_s.at[side, k], wq_r.at[side, k + 1])
        mine = wt.at[side, :, c]
        send(mine, mine, wc_s.at[side], wc_r.at[side], core_peer)

    def w_done(side):
        arrive(wt.at[side, :, 1 - c], wc_s.at[side], wc_r.at[side])

    def kv_on(h):
        slot = kv.at[h, :, x, 1 - zb, c]
        arrive(slot, kh_s.at[h], kh_r.at[h])
        for k in range(3):
            send(slot, slot, kf_s.at[h, k], kf_r.at[h, x], x_peers[k])

    def kv_core():
        for k in range(3):
            there = kv.at[:, :, x_at[k], zb, c]
            arrive(there, kx_s.at[k], kx_r.at[x_at[k]])
        all_x = kv.at[:, :, :, zb, c]
        send(all_x, all_x, kc_s.at[0], kc_r.at[0], core_peer)

    def kv_core_on(h):
        for k in range(3):
            slot = kv.at[h, :, x_at[k], 1 - zb, c]
            arrive(slot, kf_s.at[h, k], kf_r.at[h, x_at[k]])
        slot = kv.at[h, :, :, 1 - zb, c]
        send(slot, slot, kc_s.at[1 + h], kc_r.at[1 + h], core_peer)

    def ready():
        for k in range(3):
            arrive(q_all.at[q_at[k]], q_s.at[k], q_r.at[q_at[k]])
        for ld in [ld_text, ld_bias, ld_gate] + ld_stale:
            ld.wait()
        all_x = kv.at[:, :, :, zb, 1 - c]
        arrive(all_x, kc_s.at[0], kc_r.at[0])

    scale = HD**-0.5
    tokens = QUAD * rows
    keys = NX * 2 * NC * rows
    lane = lax.broadcasted_iota(jnp.int32, (tokens, HD), 1)
    first_row = lax.broadcasted_iota(jnp.int32, (STATS, HD), 0)
    first = (first_row == lax.broadcasted_iota(jnp.int32, (STATS, HD), 1)).astype(F32).astype(BF)

    def attend(h):
        slot = kv.at[h, :, :, 1 - zb, 1 - c]
        arrive(slot, kc_s.at[1 + h], kc_r.at[1 + h])
        cut = slice(h * HD, (h + 1) * HD)
        q = q_all[:, :, cut].reshape(tokens, HD)
        k_img = jnp.concatenate([stale_v[0, :, :, :, cut].reshape(keys, HD), kv[h, 0].reshape(keys, HD)], axis=1)
        v_img = jnp.concatenate([stale_v[1, :, :, :, cut].reshape(keys, HD), kv[h, 1].reshape(keys, HD)], axis=1)
        s_img = lax.dot_general(jnp.concatenate([q, q], axis=1), k_img, NT, preferred_element_type=F32)
        s_txt = lax.dot_general(q, text_v[0, :, cut], NT, preferred_element_type=F32)
        peak = jnp.maximum(jnp.max(s_img, axis=1, keepdims=True), jnp.max(s_txt, axis=1, keepdims=True))
        w_img = jnp.exp((s_img - peak) * scale).astype(BF)
        w_txt = jnp.exp((s_txt - peak) * scale).astype(BF)
        total = jnp.sum(w_img.astype(F32), axis=1, keepdims=True) + jnp.sum(w_txt.astype(F32), axis=1, keepdims=True)
        o_img = lax.dot_general(w_img, v_img, NN, preferred_element_type=F32)
        o_txt = lax.dot_general(w_txt, text_v[1, :, cut], NN, preferred_element_type=F32)
        o = (o_img[:, :HD] + o_img[:, HD:] + o_txt) / total
        stats = jnp.where(lane < 3, peak, total)
        third = lax.rem(lane, 3)
        top = stats.astype(BF).astype(F32)
        mid = (stats - top).astype(BF).astype(F32)
        low = stats - top - mid
        terms = jnp.where(third == 0, top, jnp.where(third == 1, mid, low))
        terms = terms.astype(BF)
        o_send[h, :, :rows] = o.astype(BF).reshape(QUAD, rows, HD)
        for v in range(QUAD):
            turned = lax.dot_general(first, terms[v * rows : (v + 1) * rows], NT, preferred_element_type=F32)
            o_send[h, v, rows:, :rows] = turned.astype(BF)
        for k in range(3):
            send(o_send.at[h, q_at[k]], o_recv.at[h, zq], o_s.at[h, k], o_r.at[h, zq], q_peers[k])

    pick_row = lax.broadcasted_iota(jnp.int32, (STATS, 2 * HD), 0)
    pick_col = lax.broadcasted_iota(jnp.int32, (STATS, 2 * HD), 1)
    pick = (lax.div(pick_row, 3) == lax.div(pick_col, HD)).astype(F32).astype(BF)

    def combine(h):
        o_recv[h, zq] = o_send[h, zq]
        for k in range(3):
            arrive(o_recv.at[h, q_at[k]], o_s.at[h, k], o_r.at[h, q_at[k]])
        wide = [
            lax.dot_general(o_recv[h, v, rows:, :rows], pick, TN, preferred_element_type=F32) for v in range(QUAD)
        ]
        peak = jnp.maximum(jnp.maximum(wide[0], wide[1]), jnp.maximum(wide[2], wide[3]))[:, :HD]
        shares = [jnp.exp((w[:, :HD] - peak) * scale) * w[:, HD:] for w in wide]
        mix = sum(shares[v] * o_recv[h, v, :rows].astype(F32) for v in range(QUAD)) / sum(shares)
        a_all[h, x] = mix.astype(BF)
        for k in range(3):
            send(a_all.at[h, x], a_all.at[h, x], a_s.at[h, k], a_r.at[h, x], x_peers[k])

    kv_half(0)
    kv_x()
    kv_half(1)
    kv_half(2)
    q_quad()
    kv_on(0)
    w_half()
    kv_core()
    kv_on(1)
    kv_on(2)
    kv_core_on(0)
    w_got_half()
    w_quad(far)
    kv_core_on(1)
    ready()
    kv_core_on(2)
    attend(0)
    attend(1)
    attend(2)
    combine(0)
    w_core(far)
    combine(1)
    w_quad(near)
    combine(2)

    for h in range(heads):
        for k in range(3):
            arrive(a_all.at[h, x_at[k]], a_s.at[h, k], a_r.at[h, x_at[k]])
    attended = jnp.concatenate([a_all[h].reshape(NX * rows, HD) for h in range(heads)], axis=1)

    def home(half):
        return pltpu.make_async_remote_copy(
            src_ref=p_send.at[half, x], dst_ref=p_recv.at[half, y], send_sem=p_s.at[half, 3], recv_sem=p_r.at[half, y],
            device_id=feature_home, device_id_type=MESH,
        )

    def project(half):
        side = near if half else far
        pieces = [wt[side, lax.rem(v + QUAD - zq, QUAD)].reshape(NC * rows, width) for v in range(QUAD)]
        term = lax.dot_general(attended, jnp.concatenate(pieces, axis=0), NT, preferred_element_type=F32)
        p_send[half] = term.astype(BF).reshape(NX, rows, width)

    def share(half):
        for k in range(3):
            send(p_send.at[half, x_at[k]], p_recv.at[half, y], p_s.at[half, k], p_r.at[half, y], feature_peers[k])

        @pl.when(away)
        def _():
            home(half).start()

        @pl.when(jnp.logical_not(away))
        def _():
            p_recv[half, y] = p_send[half, x]

    def gather(half):
        for k in range(3):
            arrive(p_recv.at[half, y_at[k]], p_s.at[half, k], p_r.at[half, y_at[k]])

        @pl.when(away)
        def _():
            home(half).wait_recv()

        return jnp.sum(p_recv[half].astype(F32), axis=0)

    w_done(far)
    project(0)
    share(0)
    w_core(near)
    w_done(near)
    project(1)
    z_send[...] = gather(0).astype(BF)
    pl.semaphore_wait(entered, 1)
    send(z_send, z_recv, zz_s, zz_r, zh_peer)
    share(1)
    rest = gather(1) + bias_v[...].reshape(1, width)
    arrive(z_recv, zz_s, zz_r)
    out_ref[...] = (gate_v[...].reshape(1, width) * (rest + z_recv[...].astype(F32))).astype(BF)
    for cp in pending:
        cp.wait_send()

    @pl.when(away)
    def _():
        for half in range(2):
            home(half).wait_send()


def body(queries, stale_kv, codes, exponents, text_kv, out_weight, out_bias, out_gate):
    rows, width = queries.shape
    heads = width // HD
    dma = pltpu.SemaphoreType.DMA
    any_spec = pl.BlockSpec(memory_space=pl.ANY)
    return pl.pallas_call(
        kernel,
        out_shape=jax.ShapeDtypeStruct((rows, width), BF),
        in_specs=[any_spec] * 8,
        out_specs=pl.BlockSpec(memory_space=pltpu.VMEM),
        scratch_shapes=[
            pltpu.VMEM(codes.shape, jnp.int32),
            pltpu.VMEM((heads, 2, rows), jnp.int32),
            pltpu.VMEM((width,), F32),
            pltpu.VMEM((width,), F32),
            pltpu.VMEM((2, NX, 2, NC * rows, width), BF),
            pltpu.VMEM((2, text_kv.shape[1] // QUAD, width), BF),
            pltpu.VMEM((QUAD, rows, width), BF),
            pltpu.VMEM((heads, 2, NX, 2, NC, rows, HD), BF),
            pltpu.VMEM((2, QUAD, NC, rows, width), BF),
            pltpu.VMEM((heads, QUAD, rows + STATS, HD), BF),
            pltpu.VMEM((heads, QUAD, rows + STATS, HD), BF),
            pltpu.VMEM((heads, NX, rows, HD), BF),
            pltpu.VMEM((2, NX, rows, width), BF),
            pltpu.VMEM((2, NY, rows, width), BF),
            pltpu.VMEM((rows, width), BF),
            pltpu.VMEM((rows, width), BF),
            dma((15,)),
            dma((3,)), dma((QUAD,)),
            dma((heads,)), dma((heads,)),
            dma((3,)), dma((NX,)),
            dma((heads, 3)), dma((heads, NX)),
            dma((heads + 1,)), dma((heads + 1,)),
            dma(()), dma(()),
            dma((2, 3)), dma((2, QUAD)),
            dma((2,)), dma((2,)),
            dma((heads, 3)), dma((heads, QUAD)),
            dma((heads, 3)), dma((heads, NX)),
            dma((2, 4)), dma((2, NY)),
            dma(()), dma(()),
            pltpu.SemaphoreType.REGULAR,
        ],
        compiler_params=pltpu.CompilerParams(
            collective_id=0, has_side_effects=True, vmem_limit_bytes=60 * 1024 * 1024
        ),
        cost_estimate=pl.CostEstimate(flops=640_000_000, bytes_accessed=4_000_000, transcendentals=520_000),
        name="joint_attention",
    )(
        queries, stale_kv, codes, exponents.transpose(2, 0, 1), text_kv, out_weight.T,
        out_bias, out_gate,
    )


def solution(mesh):
    placed = (
        P("patch", "head"),
        P(None, None, "head"),
        P(None, "patch", "head"),
        P(None, "patch", "head"),
        P(None, None, "head"),
        P("head", "patch"),
        P("head"),
        P("head"),
    )
    return jax.shard_map(
        body, mesh=mesh, in_specs=placed, out_specs=P("patch", "head"), check_vma=False
    )
```

```python
import jax
import jax.numpy as jnp
from jax import lax
from jax.experimental import pallas as pl
from jax.experimental.pallas import tpu as pltpu
from jax.sharding import PartitionSpec as P

HD = 128
NX, NZ, NC, NY, NH = 4, 8, 2, 4, 2
QUAD = 4
BF = jnp.bfloat16
F32 = jnp.float32
MESH = pl.DeviceIdType.MESH
NT = (((1,), (1,)), ((), ()))
NN = (((1,), (0,)), ((), ()))
TN = (((0,), (0,)), ((), ()))
STATS = 16


def kernel(
    q_hbm, stale_hbm, codes_hbm, exps_hbm, text_hbm, w_hbm, bias_hbm, gate_hbm,
    out_ref,
    codes_v, exps_v, bias_v, gate_v, stale_v, text_v,
    q_all, kv, wt, o_send, o_recv, a_all, p_send, p_recv, z_send, z_recv,
    lsem, q_s, q_r, kh_s, kh_r, kx_s, kx_r, kf_s, kf_r, kc_s, kc_r,
    wh_s, wh_r, wq_s, wq_r, wc_s, wc_r, o_s, o_r, a_s, a_r, p_s, p_r, zz_s, zz_r, entered,
):
    rows, width = q_hbm.shape
    heads = width // HD
    text_rows = text_hbm.shape[1] // QUAD
    p = lax.axis_index("patch")
    hd = lax.axis_index("head")
    x = lax.div(p, NZ * NC)
    z = lax.rem(lax.div(p, NC), NZ)
    c = lax.rem(p, NC)
    y = lax.div(hd, NH)
    zh = lax.rem(hd, NH)
    zb = lax.div(z, QUAD)
    zq = lax.rem(z, QUAD)
    far, near = 1 - zh, zh

    def dev(xx=x, z_=z, cc=c, yy=y, hh=zh):
        return (xx * (NZ * NC) + z_ * NC + cc, yy * NH + hh)

    def ring(k):
        at = lax.rem(zh * NZ + z + k, NZ * NH)
        return dev(z_=lax.rem(at, NZ), hh=lax.div(at, NZ))

    core_peer = dev(cc=1 - c)
    half_peer = dev(z_=(1 - zb) * QUAD + zq)
    zh_peer = dev(hh=1 - zh)
    x_at = [lax.rem(x + k, NX) for k in (1, 2, 3)]
    y_at = [lax.rem(y + k, NY) for k in (1, 2, 3)]
    q_at = [lax.rem(zq + k, QUAD) for k in (1, 2, 3)]
    x_peers = [dev(xx=v) for v in x_at]
    feature_peers = [dev(xx=v, yy=x) for v in x_at]
    feature_home = dev(yy=x)
    feature_from = [dev(xx=y, yy=v) for v in y_at]
    away = x != y
    feature_near = dev(xx=y, cc=jnp.where(away, c, 1 - c))
    q_peers = [dev(z_=zb * QUAD + v) for v in q_at]

    pending = []

    def send(src, dst, s, r, to):
        cp = pltpu.make_async_remote_copy(
            src_ref=src, dst_ref=dst, send_sem=s, recv_sem=r, device_id=to, device_id_type=MESH
        )
        cp.start()
        pending.append(cp)

    def arrive(dst, s, r):
        pltpu.make_async_remote_copy(
            src_ref=dst, dst_ref=dst, send_sem=s, recv_sem=r, device_id=core_peer, device_id_type=MESH
        ).wait_recv()

    barrier = pltpu.get_barrier_semaphore()
    everyone = [ring(4), ring(NZ * NH - 4), core_peer] + x_peers + q_peers
    for peer in everyone + feature_from + [feature_near]:
        pl.semaphore_signal(barrier, inc=1, device_id=peer, device_id_type=MESH)

    ld_codes = pltpu.make_async_copy(codes_hbm, codes_v, lsem.at[0])
    ld_exps = pltpu.make_async_copy(exps_hbm, exps_v, lsem.at[1])
    ld_w = pltpu.make_async_copy(w_hbm, wt.at[zb, 0, c], lsem.at[2])
    ld_q = pltpu.make_async_copy(q_hbm, q_all.at[zq], lsem.at[3])
    ld_text = pltpu.make_async_copy(text_hbm.at[:, pl.ds(zq * text_rows, text_rows)], text_v, lsem.at[4])
    ld_bias = pltpu.make_async_copy(bias_hbm, bias_v, lsem.at[5])
    ld_gate = pltpu.make_async_copy(gate_hbm, gate_v, lsem.at[6])
    ld_stale = [
        pltpu.make_async_copy(
            stale_hbm.at[:, pl.ds((xx * NZ + b * QUAD + zq) * NC * rows, NC * rows)],
            stale_v.at[:, xx, b], lsem.at[7 + xx * 2 + b],
        )
        for xx in range(NX) for b in range(2)
    ]
    for ld in [ld_codes, ld_exps, ld_w, ld_q, ld_text, ld_bias, ld_gate] + ld_stale:
        ld.start()

    diagonal = lax.broadcasted_iota(jnp.int32, (rows, rows), 0) == lax.broadcasted_iota(jnp.int32, (rows, rows), 1)
    ones = jnp.ones((rows, HD), BF)
    ld_codes.wait()
    ld_exps.wait()
    for h in range(heads):
        code = codes_v[:, :, h * HD : (h + 1) * HD]
        for kind in range(2):
            step = jnp.left_shift(jnp.int32(1), exps_v[h, kind : kind + 1] + 9).astype(F32) * (2.0**-9)
            spread = jnp.where(diagonal, step, 0.0).astype(BF)
            step = lax.dot_general(spread, ones, NN, preferred_element_type=F32)
            kv[h, kind, x, zb, c] = (code[kind].astype(F32) * step).astype(BF)
    ld_w.wait()
    ld_q.wait()

    pl.semaphore_wait(barrier, len(everyone) + 4)
    pl.semaphore_signal(entered, inc=1, device_id=ring(4), device_id_type=MESH)

    def kv_half(h):
        mine = kv.at[h, :, x, zb, c]
        send(mine, mine, kh_s.at[h], kh_r.at[h], half_peer)

    def kv_x():
        for k in range(3):
            mine = kv.at[:, :, x, zb, c]
            send(mine, mine, kx_s.at[k], kx_r.at[x], x_peers[k])

    def q_quad():
        for k in range(3):
            send(q_all.at[zq], q_all.at[zq], q_s.at[k], q_r.at[zq], q_peers[k])

    own_w = wt.at[zb, 0, c]
    half_w = wt.at[1 - zb, 0, c]

    def w_half():
        send(own_w, own_w, wh_s, wh_r, half_peer)

    def w_got_half():
        arrive(half_w, wh_s, wh_r)

    def w_quad(side):
        for k in range(3):
            send(wt.at[side, 0, c], wt.at[side, 3 - k, c], wq_s.at[side, k], wq_r.at[side, 3 - k], q_peers[k])

    def w_core(side):
        for k in range(3):
            arrive(wt.at[side, k + 1, c], wq_s.at[side, k], wq_r.at[side, k + 1])
        mine = wt.at[side, :, c]
        send(mine, mine, wc_s.at[side], wc_r.at[side], core_peer)

    def w_done(side):
        arrive(wt.at[side, :, 1 - c], wc_s.at[side], wc_r.at[side])

    def kv_on(h):
        slot = kv.at[h, :, x, 1 - zb, c]
        arrive(slot, kh_s.at[h], kh_r.at[h])
        for k in range(3):
            send(slot, slot, kf_s.at[h, k], kf_r.at[h, x], x_peers[k])

    def kv_core():
        for k in range(3):
            there = kv.at[:, :, x_at[k], zb, c]
            arrive(there, kx_s.at[k], kx_r.at[x_at[k]])
        all_x = kv.at[:, :, :, zb, c]
        send(all_x, all_x, kc_s.at[0], kc_r.at[0], core_peer)

    def kv_core_on(h):
        for k in range(3):
            slot = kv.at[h, :, x_at[k], 1 - zb, c]
            arrive(slot, kf_s.at[h, k], kf_r.at[h, x_at[k]])
        slot = kv.at[h, :, :, 1 - zb, c]
        send(slot, slot, kc_s.at[1 + h], kc_r.at[1 + h], core_peer)

    def ready():
        for k in range(3):
            arrive(q_all.at[q_at[k]], q_s.at[k], q_r.at[q_at[k]])
        for ld in [ld_text, ld_bias, ld_gate] + ld_stale:
            ld.wait()
        all_x = kv.at[:, :, :, zb, 1 - c]
        arrive(all_x, kc_s.at[0], kc_r.at[0])

    scale = HD**-0.5
    tokens = QUAD * rows
    keys = NX * 2 * NC * rows
    lane = lax.broadcasted_iota(jnp.int32, (tokens, HD), 1)
    first_row = lax.broadcasted_iota(jnp.int32, (STATS, HD), 0)
    first = (first_row == lax.broadcasted_iota(jnp.int32, (STATS, HD), 1)).astype(F32).astype(BF)

    def attend(h):
        slot = kv.at[h, :, :, 1 - zb, 1 - c]
        arrive(slot, kc_s.at[1 + h], kc_r.at[1 + h])
        cut = slice(h * HD, (h + 1) * HD)
        q = q_all[:, :, cut].reshape(tokens, HD)
        k_img = jnp.concatenate([stale_v[0, :, :, :, cut].reshape(keys, HD), kv[h, 0].reshape(keys, HD)], axis=1)
        v_img = jnp.concatenate([stale_v[1, :, :, :, cut].reshape(keys, HD), kv[h, 1].reshape(keys, HD)], axis=1)
        s_img = lax.dot_general(jnp.concatenate([q, q], axis=1), k_img, NT, preferred_element_type=F32)
        s_txt = lax.dot_general(q, text_v[0, :, cut], NT, preferred_element_type=F32)
        peak = jnp.maximum(jnp.max(s_img, axis=1, keepdims=True), jnp.max(s_txt, axis=1, keepdims=True))
        w_img = jnp.exp((s_img - peak) * scale).astype(BF)
        w_txt = jnp.exp((s_txt - peak) * scale).astype(BF)
        total = jnp.sum(w_img.astype(F32), axis=1, keepdims=True) + jnp.sum(w_txt.astype(F32), axis=1, keepdims=True)
        o_img = lax.dot_general(w_img, v_img, NN, preferred_element_type=F32)
        o_txt = lax.dot_general(w_txt, text_v[1, :, cut], NN, preferred_element_type=F32)
        o = (o_img[:, :HD] + o_img[:, HD:] + o_txt) / total
        stats = jnp.where(lane < 3, peak, total)
        third = lax.rem(lane, 3)
        top = stats.astype(BF).astype(F32)
        mid = (stats - top).astype(BF).astype(F32)
        low = stats - top - mid
        terms = jnp.where(third == 0, top, jnp.where(third == 1, mid, low))
        terms = terms.astype(BF)
        o_send[h, :, :rows] = o.astype(BF).reshape(QUAD, rows, HD)
        for v in range(QUAD):
            turned = lax.dot_general(first, terms[v * rows : (v + 1) * rows], NT, preferred_element_type=F32)
            o_send[h, v, rows:, :rows] = turned.astype(BF)
        for k in range(3):
            send(o_send.at[h, q_at[k]], o_recv.at[h, zq], o_s.at[h, k], o_r.at[h, zq], q_peers[k])

    pick_row = lax.broadcasted_iota(jnp.int32, (STATS, 2 * HD), 0)
    pick_col = lax.broadcasted_iota(jnp.int32, (STATS, 2 * HD), 1)
    pick = (lax.div(pick_row, 3) == lax.div(pick_col, HD)).astype(F32).astype(BF)

    def combine(h):
        o_recv[h, zq] = o_send[h, zq]
        for k in range(3):
            arrive(o_recv.at[h, q_at[k]], o_s.at[h, k], o_r.at[h, q_at[k]])
        wide = [
            lax.dot_general(o_recv[h, v, rows:, :rows], pick, TN, preferred_element_type=F32) for v in range(QUAD)
        ]
        peak = jnp.maximum(jnp.maximum(wide[0], wide[1]), jnp.maximum(wide[2], wide[3]))[:, :HD]
        shares = [jnp.exp((w[:, :HD] - peak) * scale) * w[:, HD:] for w in wide]
        mix = sum(shares[v] * o_recv[h, v, :rows].astype(F32) for v in range(QUAD)) / sum(shares)
        a_all[h, x] = mix.astype(BF)
        for k in range(3):
            send(a_all.at[h, x], a_all.at[h, x], a_s.at[h, k], a_r.at[h, x], x_peers[k])

    kv_half(0)
    kv_x()
    kv_half(1)
    kv_half(2)
    q_quad()
    kv_on(0)
    w_half()
    kv_core()
    kv_on(1)
    kv_on(2)
    kv_core_on(0)
    w_got_half()
    w_quad(far)
    kv_core_on(1)
    ready()
    kv_core_on(2)
    attend(0)
    attend(1)
    attend(2)
    combine(0)
    w_core(far)
    combine(1)
    w_quad(near)
    combine(2)

    for h in range(heads):
        for k in range(3):
            arrive(a_all.at[h, x_at[k]], a_s.at[h, k], a_r.at[h, x_at[k]])
    attended = jnp.concatenate([a_all[h].reshape(NX * rows, HD) for h in range(heads)], axis=1)

    def home(half):
        return pltpu.make_async_remote_copy(
            src_ref=p_send.at[half, x], dst_ref=p_recv.at[half, y], send_sem=p_s.at[half, 3], recv_sem=p_r.at[half, y],
            device_id=feature_home, device_id_type=MESH,
        )

    def project(half):
        side = near if half else far
        pieces = [wt[side, lax.rem(v + QUAD - zq, QUAD)].reshape(NC * rows, width) for v in range(QUAD)]
        term = lax.dot_general(attended, jnp.concatenate(pieces, axis=0), NT, preferred_element_type=F32)
        p_send[half] = term.astype(BF).reshape(NX, rows, width)

    def share(half):
        for k in range(3):
            send(p_send.at[half, x_at[k]], p_recv.at[half, y], p_s.at[half, k], p_r.at[half, y], feature_peers[k])

        @pl.when(away)
        def _():
            home(half).start()

        @pl.when(jnp.logical_not(away))
        def _():
            p_recv[half, y] = p_send[half, x]

    def gather(half):
        for k in range(3):
            arrive(p_recv.at[half, y_at[k]], p_s.at[half, k], p_r.at[half, y_at[k]])

        @pl.when(away)
        def _():
            home(half).wait_recv()

        return jnp.sum(p_recv[half].astype(F32), axis=0)

    w_done(far)
    project(0)
    share(0)
    w_core(near)
    z_send[...] = gather(0).astype(BF)
    pl.semaphore_wait(entered, 1)
    send(z_send, z_recv, zz_s, zz_r, zh_peer)
    w_done(near)
    project(1)
    share(1)
    rest = gather(1) + bias_v[...].reshape(1, width)
    arrive(z_recv, zz_s, zz_r)
    out_ref[...] = (gate_v[...].reshape(1, width) * (rest + z_recv[...].astype(F32))).astype(BF)
    for cp in pending:
        cp.wait_send()

    @pl.when(away)
    def _():
        for half in range(2):
            home(half).wait_send()


def body(queries, stale_kv, codes, exponents, text_kv, out_weight, out_bias, out_gate):
    rows, width = queries.shape
    heads = width // HD
    dma = pltpu.SemaphoreType.DMA
    any_spec = pl.BlockSpec(memory_space=pl.ANY)
    return pl.pallas_call(
        kernel,
        out_shape=pltpu.VMEM((rows, width), BF),
        in_specs=[any_spec] * 8,
        out_specs=pl.BlockSpec(memory_space=pltpu.VMEM),
        scratch_shapes=[
            pltpu.VMEM(codes.shape, jnp.int32),
            pltpu.VMEM((heads, 2, rows), jnp.int32),
            pltpu.VMEM((width,), F32),
            pltpu.VMEM((width,), F32),
            pltpu.VMEM((2, NX, 2, NC * rows, width), BF),
            pltpu.VMEM((2, text_kv.shape[1] // QUAD, width), BF),
            pltpu.VMEM((QUAD, rows, width), BF),
            pltpu.VMEM((heads, 2, NX, 2, NC, rows, HD), BF),
            pltpu.VMEM((2, QUAD, NC, rows, width), BF),
            pltpu.VMEM((heads, QUAD, rows + STATS, HD), BF),
            pltpu.VMEM((heads, QUAD, rows + STATS, HD), BF),
            pltpu.VMEM((heads, NX, rows, HD), BF),
            pltpu.VMEM((2, NX, rows, width), BF),
            pltpu.VMEM((2, NY, rows, width), BF),
            pltpu.VMEM((rows, width), BF),
            pltpu.VMEM((rows, width), BF),
            dma((15,)),
            dma((3,)), dma((QUAD,)),
            dma((heads,)), dma((heads,)),
            dma((3,)), dma((NX,)),
            dma((heads, 3)), dma((heads, NX)),
            dma((heads + 1,)), dma((heads + 1,)),
            dma(()), dma(()),
            dma((2, 3)), dma((2, QUAD)),
            dma((2,)), dma((2,)),
            dma((heads, 3)), dma((heads, QUAD)),
            dma((heads, 3)), dma((heads, NX)),
            dma((2, 4)), dma((2, NY)),
            dma(()), dma(()),
            pltpu.SemaphoreType.REGULAR,
        ],
        compiler_params=pltpu.CompilerParams(
            collective_id=0, has_side_effects=True, vmem_limit_bytes=60 * 1024 * 1024
        ),
        cost_estimate=pl.CostEstimate(flops=640_000_000, bytes_accessed=4_000_000, transcendentals=520_000),
        name="joint_attention",
    )(
        queries, stale_kv, codes, exponents.transpose(2, 0, 1), text_kv, out_weight.T,
        out_bias, out_gate,
    )


def solution(mesh):
    placed = (
        P("patch", "head"),
        P(None, None, "head"),
        P(None, "patch", "head"),
        P(None, "patch", "head"),
        P(None, None, "head"),
        P("head", "patch"),
        P("head"),
        P("head"),
    )
    return jax.shard_map(
        body, mesh=mesh, in_specs=placed, out_specs=P("patch", "head"), check_vma=False
    )
```

```python
import jax
import jax.numpy as jnp
from jax import lax
from jax.experimental import pallas as pl
from jax.experimental.pallas import tpu as pltpu
from jax.sharding import PartitionSpec as P

HD = 128
NX, NZ, NC, NY, NH = 4, 8, 2, 4, 2
QUAD = 4
BF = jnp.bfloat16
F32 = jnp.float32
MESH = pl.DeviceIdType.MESH
NT = (((1,), (1,)), ((), ()))
NN = (((1,), (0,)), ((), ()))
TN = (((0,), (0,)), ((), ()))
STATS = 16


def kernel(
    q_hbm, stale_hbm, codes_hbm, exps_hbm, text_hbm, w_hbm, bias_hbm, gate_hbm,
    out_ref,
    codes_v, exps_v, bias_v, gate_v, stale_v, text_v,
    q_all, kv, wt, o_send, o_recv, a_all, p_send, p_recv, z_send, z_recv,
    lsem, q_s, q_r, kh_s, kh_r, kx_s, kx_r, kf_s, kf_r, kc_s, kc_r,
    wh_s, wh_r, wq_s, wq_r, wc_s, wc_r, o_s, o_r, a_s, a_r, p_s, p_r, zz_s, zz_r, entered,
):
    rows, width = q_hbm.shape
    heads = width // HD
    text_rows = text_hbm.shape[1] // QUAD
    p = lax.axis_index("patch")
    hd = lax.axis_index("head")
    x = lax.div(p, NZ * NC)
    z = lax.rem(lax.div(p, NC), NZ)
    c = lax.rem(p, NC)
    y = lax.div(hd, NH)
    zh = lax.rem(hd, NH)
    zb = lax.div(z, QUAD)
    zq = lax.rem(z, QUAD)
    far, near = 1 - zh, zh

    def dev(xx=x, z_=z, cc=c, yy=y, hh=zh):
        return (xx * (NZ * NC) + z_ * NC + cc, yy * NH + hh)

    def ring(k):
        at = lax.rem(zh * NZ + z + k, NZ * NH)
        return dev(z_=lax.rem(at, NZ), hh=lax.div(at, NZ))

    core_peer = dev(cc=1 - c)
    half_peer = dev(z_=(1 - zb) * QUAD + zq)
    zh_peer = dev(hh=1 - zh)
    x_at = [lax.rem(x + k, NX) for k in (1, 2, 3)]
    y_at = [lax.rem(y + k, NY) for k in (1, 2, 3)]
    q_at = [lax.rem(zq + k, QUAD) for k in (1, 2, 3)]
    x_peers = [dev(xx=v) for v in x_at]
    feature_peers = [dev(xx=v, yy=x) for v in x_at]
    feature_home = dev(yy=x)
    feature_from = [dev(xx=y, yy=v) for v in y_at]
    away = x != y
    feature_near = dev(xx=y, cc=jnp.where(away, c, 1 - c))
    q_peers = [dev(z_=zb * QUAD + v) for v in q_at]

    pending = []

    def send(src, dst, s, r, to):
        cp = pltpu.make_async_remote_copy(
            src_ref=src, dst_ref=dst, send_sem=s, recv_sem=r, device_id=to, device_id_type=MESH
        )
        cp.start()
        pending.append(cp)

    def arrive(dst, s, r):
        pltpu.make_async_remote_copy(
            src_ref=dst, dst_ref=dst, send_sem=s, recv_sem=r, device_id=core_peer, device_id_type=MESH
        ).wait_recv()

    barrier = pltpu.get_barrier_semaphore()
    everyone = [ring(4), ring(NZ * NH - 4), core_peer] + x_peers + q_peers
    for peer in everyone + feature_from + [feature_near]:
        pl.semaphore_signal(barrier, inc=1, device_id=peer, device_id_type=MESH)

    ld_codes = pltpu.make_async_copy(codes_hbm, codes_v, lsem.at[0])
    ld_exps = pltpu.make_async_copy(exps_hbm, exps_v, lsem.at[1])
    ld_w = pltpu.make_async_copy(w_hbm, wt.at[zb, 0, c], lsem.at[2])
    ld_q = pltpu.make_async_copy(q_hbm, q_all.at[zq], lsem.at[3])
    ld_text = pltpu.make_async_copy(text_hbm.at[:, pl.ds(zq * text_rows, text_rows)], text_v, lsem.at[4])
    ld_bias = pltpu.make_async_copy(bias_hbm, bias_v, lsem.at[5])
    ld_gate = pltpu.make_async_copy(gate_hbm, gate_v, lsem.at[6])
    ld_stale = [
        pltpu.make_async_copy(
            stale_hbm.at[:, pl.ds((xx * NZ + b * QUAD + zq) * NC * rows, NC * rows)],
            stale_v.at[:, xx, b], lsem.at[7 + xx * 2 + b],
        )
        for xx in range(NX) for b in range(2)
    ]
    for ld in [ld_codes, ld_exps, ld_w, ld_q, ld_text, ld_bias, ld_gate] + ld_stale:
        ld.start()

    diagonal = lax.broadcasted_iota(jnp.int32, (rows, rows), 0) == lax.broadcasted_iota(jnp.int32, (rows, rows), 1)
    ones = jnp.ones((rows, HD), BF)
    ld_codes.wait()
    ld_exps.wait()
    for h in range(heads):
        code = codes_v[:, :, h * HD : (h + 1) * HD]
        for kind in range(2):
            step = jnp.left_shift(jnp.int32(1), exps_v[h, kind : kind + 1] + 9).astype(F32) * (2.0**-9)
            spread = jnp.where(diagonal, step, 0.0).astype(BF)
            step = lax.dot_general(spread, ones, NN, preferred_element_type=F32)
            kv[h, kind, x, zb, c] = (code[kind].astype(F32) * step).astype(BF)
    ld_w.wait()
    ld_q.wait()

    pl.semaphore_wait(barrier, len(everyone) + 4)
    pl.semaphore_signal(entered, inc=1, device_id=ring(4), device_id_type=MESH)

    def kv_half(h):
        mine = kv.at[h, :, x, zb, c]
        send(mine, mine, kh_s.at[h], kh_r.at[h], half_peer)

    def kv_x():
        for k in range(3):
            mine = kv.at[:, :, x, zb, c]
            send(mine, mine, kx_s.at[k], kx_r.at[x], x_peers[k])

    def q_quad():
        for k in range(3):
            send(q_all.at[zq], q_all.at[zq], q_s.at[k], q_r.at[zq], q_peers[k])

    own_w = wt.at[zb, 0, c]
    half_w = wt.at[1 - zb, 0, c]

    def w_half():
        send(own_w, own_w, wh_s, wh_r, half_peer)

    def w_got_half():
        arrive(half_w, wh_s, wh_r)

    def w_quad(side):
        for k in range(3):
            send(wt.at[side, 0, c], wt.at[side, 3 - k, c], wq_s.at[side, k], wq_r.at[side, 3 - k], q_peers[k])

    def w_core(side):
        for k in range(3):
            arrive(wt.at[side, k + 1, c], wq_s.at[side, k], wq_r.at[side, k + 1])
        mine = wt.at[side, :, c]
        send(mine, mine, wc_s.at[side], wc_r.at[side], core_peer)

    def w_done(side):
        arrive(wt.at[side, :, 1 - c], wc_s.at[side], wc_r.at[side])

    def kv_on(h):
        slot = kv.at[h, :, x, 1 - zb, c]
        arrive(slot, kh_s.at[h], kh_r.at[h])
        for k in range(3):
            send(slot, slot, kf_s.at[h, k], kf_r.at[h, x], x_peers[k])

    def kv_core():
        for k in range(3):
            there = kv.at[:, :, x_at[k], zb, c]
            arrive(there, kx_s.at[k], kx_r.at[x_at[k]])
        all_x = kv.at[:, :, :, zb, c]
        send(all_x, all_x, kc_s.at[0], kc_r.at[0], core_peer)

    def kv_core_on(h):
        for k in range(3):
            slot = kv.at[h, :, x_at[k], 1 - zb, c]
            arrive(slot, kf_s.at[h, k], kf_r.at[h, x_at[k]])
        slot = kv.at[h, :, :, 1 - zb, c]
        send(slot, slot, kc_s.at[1 + h], kc_r.at[1 + h], core_peer)

    def ready():
        for k in range(3):
            arrive(q_all.at[q_at[k]], q_s.at[k], q_r.at[q_at[k]])
        for ld in [ld_text, ld_bias, ld_gate] + ld_stale:
            ld.wait()
        all_x = kv.at[:, :, :, zb, 1 - c]
        arrive(all_x, kc_s.at[0], kc_r.at[0])

    scale = HD**-0.5
    tokens = QUAD * rows
    keys = NX * 2 * NC * rows
    lane = lax.broadcasted_iota(jnp.int32, (tokens, HD), 1)
    first_row = lax.broadcasted_iota(jnp.int32, (STATS, HD), 0)
    first = (first_row == lax.broadcasted_iota(jnp.int32, (STATS, HD), 1)).astype(F32).astype(BF)

    def attend(h):
        slot = kv.at[h, :, :, 1 - zb, 1 - c]
        arrive(slot, kc_s.at[1 + h], kc_r.at[1 + h])
        cut = slice(h * HD, (h + 1) * HD)
        q = q_all[:, :, cut].reshape(tokens, HD)
        k_img = jnp.concatenate([stale_v[0, :, :, :, cut].reshape(keys, HD), kv[h, 0].reshape(keys, HD)], axis=1)
        v_img = jnp.concatenate([stale_v[1, :, :, :, cut].reshape(keys, HD), kv[h, 1].reshape(keys, HD)], axis=1)
        s_img = lax.dot_general(jnp.concatenate([q, q], axis=1), k_img, NT, preferred_element_type=F32)
        s_txt = lax.dot_general(q, text_v[0, :, cut], NT, preferred_element_type=F32)
        peak = jnp.maximum(jnp.max(s_img, axis=1, keepdims=True), jnp.max(s_txt, axis=1, keepdims=True))
        w_img = jnp.exp((s_img - peak) * scale).astype(BF)
        w_txt = jnp.exp((s_txt - peak) * scale).astype(BF)
        total = jnp.sum(w_img.astype(F32), axis=1, keepdims=True) + jnp.sum(w_txt.astype(F32), axis=1, keepdims=True)
        o_img = lax.dot_general(w_img, v_img, NN, preferred_element_type=F32)
        o_txt = lax.dot_general(w_txt, text_v[1, :, cut], NN, preferred_element_type=F32)
        o = (o_img[:, :HD] + o_img[:, HD:] + o_txt) / total
        stats = jnp.where(lane < 3, peak, total)
        third = lax.rem(lane, 3)
        top = stats.astype(BF).astype(F32)
        mid = (stats - top).astype(BF).astype(F32)
        low = stats - top - mid
        terms = jnp.where(third == 0, top, jnp.where(third == 1, mid, low))
        terms = terms.astype(BF)
        o_send[h, :, :rows] = o.astype(BF).reshape(QUAD, rows, HD)
        for v in range(QUAD):
            turned = lax.dot_general(first, terms[v * rows : (v + 1) * rows], NT, preferred_element_type=F32)
            o_send[h, v, rows:, :rows] = turned.astype(BF)
        for k in range(3):
            send(o_send.at[h, q_at[k]], o_recv.at[h, zq], o_s.at[h, k], o_r.at[h, zq], q_peers[k])

    pick_row = lax.broadcasted_iota(jnp.int32, (STATS, 2 * HD), 0)
    pick_col = lax.broadcasted_iota(jnp.int32, (STATS, 2 * HD), 1)
    pick = (lax.div(pick_row, 3) == lax.div(pick_col, HD)).astype(F32).astype(BF)

    def combine(h):
        o_recv[h, zq] = o_send[h, zq]
        for k in range(3):
            arrive(o_recv.at[h, q_at[k]], o_s.at[h, k], o_r.at[h, q_at[k]])
        wide = [
            lax.dot_general(o_recv[h, v, rows:, :rows], pick, TN, preferred_element_type=F32) for v in range(QUAD)
        ]
        peak = jnp.maximum(jnp.maximum(wide[0], wide[1]), jnp.maximum(wide[2], wide[3]))[:, :HD]
        shares = [jnp.exp((w[:, :HD] - peak) * scale) * w[:, HD:] for w in wide]
        mix = sum(shares[v] * o_recv[h, v, :rows].astype(F32) for v in range(QUAD)) / sum(shares)
        a_all[h, x] = mix.astype(BF)
        for k in range(3):
            send(a_all.at[h, x], a_all.at[h, x], a_s.at[h, k], a_r.at[h, x], x_peers[k])

    kv_half(0)
    kv_x()
    kv_half(1)
    kv_half(2)
    q_quad()
    kv_core()
    kv_on(0)
    w_half()
    kv_on(1)
    kv_on(2)
    kv_core_on(0)
    w_got_half()
    w_quad(far)
    kv_core_on(1)
    ready()
    kv_core_on(2)
    attend(0)
    attend(1)
    attend(2)
    combine(0)
    w_core(far)
    combine(1)
    w_quad(near)
    combine(2)

    for h in range(heads):
        for k in range(3):
            arrive(a_all.at[h, x_at[k]], a_s.at[h, k], a_r.at[h, x_at[k]])
    attended = jnp.concatenate([a_all[h].reshape(NX * rows, HD) for h in range(heads)], axis=1)

    def columns(t):
        return (1, pl.ds(0, width)) if t == heads else (0, pl.ds(t * HD, HD))

    def home(t):
        half, span = columns(t)
        return pltpu.make_async_remote_copy(
            src_ref=p_send.at[half, x, :, span], dst_ref=p_recv.at[half, y, :, span],
            send_sem=p_s.at[t, 3], recv_sem=p_r.at[t, y], device_id=feature_home, device_id_type=MESH,
        )

    def project(t):
        half, span = columns(t)
        for k in (1, 0, 2):
            send(p_send.at[half, x_at[k], :, span], p_recv.at[half, y, :, span], p_s.at[t, k], p_r.at[t, y], feature_peers[k])

        @pl.when(away)
        def _():
            home(t).start()

        @pl.when(jnp.logical_not(away))
        def _():
            p_recv[half, y, :, span] = p_send[half, x, :, span]

    def product(side, rows_of):
        pieces = [wt[side, lax.rem(v + QUAD - zq, QUAD)].reshape(NC * rows, width) for v in range(QUAD)]
        block = jnp.concatenate(pieces, axis=0)[rows_of]
        term = lax.dot_general(attended, block, NT, preferred_element_type=F32).astype(BF)
        return term.reshape(NX, rows, term.shape[1])

    def gather(t):
        half, span = columns(t)
        for k in range(3):
            arrive(p_recv.at[half, y_at[k], :, span], p_s.at[t, k], p_r.at[t, y_at[k]])

        @pl.when(away)
        def _():
            home(t).wait_recv()

        return jnp.sum(p_recv[half, :, :, span].astype(F32), axis=0)

    w_done(far)
    for t in range(heads):
        p_send[0, :, :, t * HD : (t + 1) * HD] = product(far, slice(t * HD, (t + 1) * HD))
        project(t)
    w_core(near)
    for t in range(heads):
        span = pl.ds(t * HD, HD)
        z_send[:, span] = gather(t).astype(BF)
        if t == 0:
            pl.semaphore_wait(entered, 1)
        send(z_send.at[:, span], z_recv.at[:, span], zz_s.at[t], zz_r.at[t], zh_peer)
    w_done(near)
    p_send[1] = product(near, slice(0, width))
    project(heads)
    rest = gather(heads) + bias_v[...].reshape(1, width)
    for t in range(heads):
        span = pl.ds(t * HD, HD)
        arrive(z_recv.at[:, span], zz_s.at[t], zz_r.at[t])
    out_ref[...] = (gate_v[...].reshape(1, width) * (rest + z_recv[...].astype(F32))).astype(BF)
    for cp in pending:
        cp.wait_send()

    @pl.when(away)
    def _():
        for t in range(heads + 1):
            home(t).wait_send()


def body(queries, stale_kv, codes, exponents, text_kv, out_weight, out_bias, out_gate):
    rows, width = queries.shape
    heads = width // HD
    dma = pltpu.SemaphoreType.DMA
    any_spec = pl.BlockSpec(memory_space=pl.ANY)
    return pl.pallas_call(
        kernel,
        out_shape=pltpu.VMEM((rows, width), BF),
        in_specs=[any_spec] * 8,
        out_specs=pl.BlockSpec(memory_space=pltpu.VMEM),
        scratch_shapes=[
            pltpu.VMEM(codes.shape, jnp.int32),
            pltpu.VMEM((heads, 2, rows), jnp.int32),
            pltpu.VMEM((width,), F32),
            pltpu.VMEM((width,), F32),
            pltpu.VMEM((2, NX, 2, NC * rows, width), BF),
            pltpu.VMEM((2, text_kv.shape[1] // QUAD, width), BF),
            pltpu.VMEM((QUAD, rows, width), BF),
            pltpu.VMEM((heads, 2, NX, 2, NC, rows, HD), BF),
            pltpu.VMEM((2, QUAD, NC, rows, width), BF),
            pltpu.VMEM((heads, QUAD, rows + STATS, HD), BF),
            pltpu.VMEM((heads, QUAD, rows + STATS, HD), BF),
            pltpu.VMEM((heads, NX, rows, HD), BF),
            pltpu.VMEM((2, NX, rows, width), BF),
            pltpu.VMEM((2, NY, rows, width), BF),
            pltpu.VMEM((rows, width), BF),
            pltpu.VMEM((rows, width), BF),
            dma((15,)),
            dma((3,)), dma((QUAD,)),
            dma((heads,)), dma((heads,)),
            dma((3,)), dma((NX,)),
            dma((heads, 3)), dma((heads, NX)),
            dma((heads + 1,)), dma((heads + 1,)),
            dma(()), dma(()),
            dma((2, 3)), dma((2, QUAD)),
            dma((2,)), dma((2,)),
            dma((heads, 3)), dma((heads, QUAD)),
            dma((heads, 3)), dma((heads, NX)),
            dma((heads + 1, 4)), dma((heads + 1, NY)),
            dma((heads,)), dma((heads,)),
            pltpu.SemaphoreType.REGULAR,
        ],
        compiler_params=pltpu.CompilerParams(
            collective_id=0, has_side_effects=True, vmem_limit_bytes=60 * 1024 * 1024
        ),
        cost_estimate=pl.CostEstimate(flops=640_000_000, bytes_accessed=4_000_000, transcendentals=520_000),
        name="joint_attention",
    )(
        queries, stale_kv, codes, exponents.transpose(2, 0, 1), text_kv, out_weight.T,
        out_bias, out_gate,
    )


def solution(mesh):
    placed = (
        P("patch", "head"),
        P(None, None, "head"),
        P(None, "patch", "head"),
        P(None, "patch", "head"),
        P(None, None, "head"),
        P("head", "patch"),
        P("head"),
        P("head"),
    )
    return jax.shard_map(
        body, mesh=mesh, in_specs=placed, out_specs=P("patch", "head"), check_vma=False
    )
```

```python
import jax
import jax.numpy as jnp
from jax import lax
from jax.experimental import pallas as pl
from jax.experimental.pallas import tpu as pltpu
from jax.sharding import PartitionSpec as P

HD = 128
NX, NZ, NC, NY, NH = 4, 8, 2, 4, 2
QUAD = 4
BF = jnp.bfloat16
F32 = jnp.float32
MESH = pl.DeviceIdType.MESH
NT = (((1,), (1,)), ((), ()))
NN = (((1,), (0,)), ((), ()))
TN = (((0,), (0,)), ((), ()))
STATS = 16


def kernel(
    q_hbm, stale_hbm, codes_hbm, exps_hbm, text_hbm, w_hbm, bias_hbm, gate_hbm,
    out_ref,
    codes_v, exps_v, bias_v, gate_v, stale_v, text_v,
    q_all, kv, wt, o_send, o_recv, a_all, p_send, p_recv, z_send, z_recv,
    lsem, q_s, q_r, kh_s, kh_r, kx_s, kx_r, kf_s, kf_r, kc_s, kc_r,
    wh_s, wh_r, wq_s, wq_r, wc_s, wc_r, o_s, o_r, a_s, a_r, p_s, p_r, zz_s, zz_r, entered,
):
    rows, width = q_hbm.shape
    heads = width // HD
    text_rows = text_hbm.shape[1] // QUAD
    p = lax.axis_index("patch")
    hd = lax.axis_index("head")
    x = lax.div(p, NZ * NC)
    z = lax.rem(lax.div(p, NC), NZ)
    c = lax.rem(p, NC)
    y = lax.div(hd, NH)
    zh = lax.rem(hd, NH)
    zb = lax.div(z, QUAD)
    zq = lax.rem(z, QUAD)
    far, near = 1 - zh, zh

    def dev(xx=x, z_=z, cc=c, yy=y, hh=zh):
        return (xx * (NZ * NC) + z_ * NC + cc, yy * NH + hh)

    def ring(k):
        at = lax.rem(zh * NZ + z + k, NZ * NH)
        return dev(z_=lax.rem(at, NZ), hh=lax.div(at, NZ))

    core_peer = dev(cc=1 - c)
    half_peer = dev(z_=(1 - zb) * QUAD + zq)
    zh_peer = dev(hh=1 - zh)
    x_at = [lax.rem(x + k, NX) for k in (1, 2, 3)]
    y_at = [lax.rem(y + k, NY) for k in (1, 2, 3)]
    q_at = [lax.rem(zq + k, QUAD) for k in (1, 2, 3)]
    x_peers = [dev(xx=v) for v in x_at]
    feature_peers = [dev(xx=v, yy=x) for v in x_at]
    feature_home = dev(yy=x)
    feature_from = [dev(xx=y, yy=v) for v in y_at]
    away = x != y
    feature_near = dev(xx=y, cc=jnp.where(away, c, 1 - c))
    q_peers = [dev(z_=zb * QUAD + v) for v in q_at]

    pending = []

    def send(src, dst, s, r, to):
        cp = pltpu.make_async_remote_copy(
            src_ref=src, dst_ref=dst, send_sem=s, recv_sem=r, device_id=to, device_id_type=MESH
        )
        cp.start()
        pending.append(cp)

    def arrive(dst, s, r):
        pltpu.make_async_remote_copy(
            src_ref=dst, dst_ref=dst, send_sem=s, recv_sem=r, device_id=core_peer, device_id_type=MESH
        ).wait_recv()

    barrier = pltpu.get_barrier_semaphore()
    everyone = [ring(4), ring(NZ * NH - 4), core_peer] + x_peers + q_peers
    for peer in everyone + feature_from + [feature_near]:
        pl.semaphore_signal(barrier, inc=1, device_id=peer, device_id_type=MESH)

    ld_codes = pltpu.make_async_copy(codes_hbm, codes_v, lsem.at[0])
    ld_exps = pltpu.make_async_copy(exps_hbm, exps_v, lsem.at[1])
    ld_w = pltpu.make_async_copy(w_hbm, wt.at[zb, 0, c], lsem.at[2])
    ld_q = pltpu.make_async_copy(q_hbm, q_all.at[zq], lsem.at[3])
    ld_text = pltpu.make_async_copy(text_hbm.at[:, pl.ds(zq * text_rows, text_rows)], text_v, lsem.at[4])
    ld_bias = pltpu.make_async_copy(bias_hbm, bias_v, lsem.at[5])
    ld_gate = pltpu.make_async_copy(gate_hbm, gate_v, lsem.at[6])
    ld_stale = [
        pltpu.make_async_copy(
            stale_hbm.at[:, pl.ds((xx * NZ + b * QUAD + zq) * NC * rows, NC * rows)],
            stale_v.at[:, xx, b], lsem.at[7 + xx * 2 + b],
        )
        for xx in range(NX) for b in range(2)
    ]
    for ld in [ld_codes, ld_exps, ld_w, ld_q, ld_text, ld_bias, ld_gate] + ld_stale:
        ld.start()

    diagonal = lax.broadcasted_iota(jnp.int32, (rows, rows), 0) == lax.broadcasted_iota(jnp.int32, (rows, rows), 1)
    ones = jnp.ones((rows, HD), BF)
    ld_codes.wait()
    ld_exps.wait()
    for h in range(heads):
        code = codes_v[:, :, h * HD : (h + 1) * HD]
        for kind in range(2):
            step = jnp.left_shift(jnp.int32(1), exps_v[h, kind : kind + 1] + 9).astype(F32) * (2.0**-9)
            spread = jnp.where(diagonal, step, 0.0).astype(BF)
            step = lax.dot_general(spread, ones, NN, preferred_element_type=F32)
            kv[h, kind, x, zb, c] = (code[kind].astype(F32) * step).astype(BF)
    ld_w.wait()
    ld_q.wait()

    pl.semaphore_wait(barrier, len(everyone) + 4)
    pl.semaphore_signal(entered, inc=1, device_id=ring(4), device_id_type=MESH)

    def kv_half(h):
        mine = kv.at[h, :, x, zb, c]
        send(mine, mine, kh_s.at[h], kh_r.at[h], half_peer)

    def kv_x():
        for k in (1, 0, 2):
            mine = kv.at[:, :, x, zb, c]
            send(mine, mine, kx_s.at[k], kx_r.at[x], x_peers[k])

    def q_quad():
        for k in range(3):
            send(q_all.at[zq], q_all.at[zq], q_s.at[k], q_r.at[zq], q_peers[k])

    own_w = wt.at[zb, 0, c]
    half_w = wt.at[1 - zb, 0, c]

    def w_half():
        send(own_w, own_w, wh_s, wh_r, half_peer)

    def w_got_half():
        arrive(half_w, wh_s, wh_r)

    def w_quad(side):
        for k in range(3):
            send(wt.at[side, 0, c], wt.at[side, 3 - k, c], wq_s.at[side, k], wq_r.at[side, 3 - k], q_peers[k])

    def w_core(side):
        for k in range(3):
            arrive(wt.at[side, k + 1, c], wq_s.at[side, k], wq_r.at[side, k + 1])
        mine = wt.at[side, :, c]
        send(mine, mine, wc_s.at[side], wc_r.at[side], core_peer)

    def w_done(side):
        arrive(wt.at[side, :, 1 - c], wc_s.at[side], wc_r.at[side])

    def kv_on(h):
        slot = kv.at[h, :, x, 1 - zb, c]
        arrive(slot, kh_s.at[h], kh_r.at[h])
        for k in (1, 0, 2):
            send(slot, slot, kf_s.at[h, k], kf_r.at[h, x], x_peers[k])

    def kv_core():
        for k in range(3):
            there = kv.at[:, :, x_at[k], zb, c]
            arrive(there, kx_s.at[k], kx_r.at[x_at[k]])
        all_x = kv.at[:, :, :, zb, c]
        send(all_x, all_x, kc_s.at[0], kc_r.at[0], core_peer)

    def kv_core_on(h):
        for k in range(3):
            slot = kv.at[h, :, x_at[k], 1 - zb, c]
            arrive(slot, kf_s.at[h, k], kf_r.at[h, x_at[k]])
        slot = kv.at[h, :, :, 1 - zb, c]
        send(slot, slot, kc_s.at[1 + h], kc_r.at[1 + h], core_peer)

    def ready():
        for k in range(3):
            arrive(q_all.at[q_at[k]], q_s.at[k], q_r.at[q_at[k]])
        for ld in [ld_text, ld_bias, ld_gate] + ld_stale:
            ld.wait()
        all_x = kv.at[:, :, :, zb, 1 - c]
        arrive(all_x, kc_s.at[0], kc_r.at[0])

    scale = HD**-0.5
    tokens = QUAD * rows
    keys = NX * 2 * NC * rows
    lane = lax.broadcasted_iota(jnp.int32, (tokens, HD), 1)
    first_row = lax.broadcasted_iota(jnp.int32, (STATS, HD), 0)
    first = (first_row == lax.broadcasted_iota(jnp.int32, (STATS, HD), 1)).astype(F32).astype(BF)

    def attend(h):
        slot = kv.at[h, :, :, 1 - zb, 1 - c]
        arrive(slot, kc_s.at[1 + h], kc_r.at[1 + h])
        cut = slice(h * HD, (h + 1) * HD)
        q = q_all[:, :, cut].reshape(tokens, HD)
        k_img = jnp.concatenate([stale_v[0, :, :, :, cut].reshape(keys, HD), kv[h, 0].reshape(keys, HD)], axis=1)
        v_img = jnp.concatenate([stale_v[1, :, :, :, cut].reshape(keys, HD), kv[h, 1].reshape(keys, HD)], axis=1)
        s_img = lax.dot_general(jnp.concatenate([q, q], axis=1), k_img, NT, preferred_element_type=F32)
        s_txt = lax.dot_general(q, text_v[0, :, cut], NT, preferred_element_type=F32)
        peak = jnp.maximum(jnp.max(s_img, axis=1, keepdims=True), jnp.max(s_txt, axis=1, keepdims=True))
        w_img = jnp.exp((s_img - peak) * scale).astype(BF)
        w_txt = jnp.exp((s_txt - peak) * scale).astype(BF)
        total = jnp.sum(w_img.astype(F32), axis=1, keepdims=True) + jnp.sum(w_txt.astype(F32), axis=1, keepdims=True)
        o_img = lax.dot_general(w_img, v_img, NN, preferred_element_type=F32)
        o_txt = lax.dot_general(w_txt, text_v[1, :, cut], NN, preferred_element_type=F32)
        o = (o_img[:, :HD] + o_img[:, HD:] + o_txt) / total
        stats = jnp.where(lane < 3, peak, total)
        third = lax.rem(lane, 3)
        top = stats.astype(BF).astype(F32)
        mid = (stats - top).astype(BF).astype(F32)
        low = stats - top - mid
        terms = jnp.where(third == 0, top, jnp.where(third == 1, mid, low))
        terms = terms.astype(BF)
        o_send[h, :, :rows] = o.astype(BF).reshape(QUAD, rows, HD)
        for v in range(QUAD):
            turned = lax.dot_general(first, terms[v * rows : (v + 1) * rows], NT, preferred_element_type=F32)
            o_send[h, v, rows:, :rows] = turned.astype(BF)
        for k in range(3):
            send(o_send.at[h, q_at[k]], o_recv.at[h, zq], o_s.at[h, k], o_r.at[h, zq], q_peers[k])

    pick_row = lax.broadcasted_iota(jnp.int32, (STATS, 2 * HD), 0)
    pick_col = lax.broadcasted_iota(jnp.int32, (STATS, 2 * HD), 1)
    pick = (lax.div(pick_row, 3) == lax.div(pick_col, HD)).astype(F32).astype(BF)

    def combine(h):
        o_recv[h, zq] = o_send[h, zq]
        for k in range(3):
            arrive(o_recv.at[h, q_at[k]], o_s.at[h, k], o_r.at[h, q_at[k]])
        wide = [
            lax.dot_general(o_recv[h, v, rows:, :rows], pick, TN, preferred_element_type=F32) for v in range(QUAD)
        ]
        peak = jnp.maximum(jnp.maximum(wide[0], wide[1]), jnp.maximum(wide[2], wide[3]))[:, :HD]
        shares = [jnp.exp((w[:, :HD] - peak) * scale) * w[:, HD:] for w in wide]
        mix = sum(shares[v] * o_recv[h, v, :rows].astype(F32) for v in range(QUAD)) / sum(shares)
        a_all[h, x] = mix.astype(BF)
        for k in (1, 0, 2):
            send(a_all.at[h, x], a_all.at[h, x], a_s.at[h, k], a_r.at[h, x], x_peers[k])

    kv_half(0)
    kv_x()
    kv_half(1)
    kv_half(2)
    q_quad()
    kv_core()
    kv_on(0)
    w_half()
    kv_on(1)
    kv_on(2)
    kv_core_on(0)
    w_got_half()
    w_quad(far)
    kv_core_on(1)
    ready()
    kv_core_on(2)
    attend(0)
    attend(1)
    attend(2)
    combine(0)
    w_core(far)
    combine(1)
    w_quad(near)
    combine(2)

    for h in range(heads):
        for k in range(3):
            arrive(a_all.at[h, x_at[k]], a_s.at[h, k], a_r.at[h, x_at[k]])
    attended = jnp.concatenate([a_all[h].reshape(NX * rows, HD) for h in range(heads)], axis=1)

    def columns(t):
        return (1, pl.ds(0, width)) if t == heads else (0, pl.ds(t * HD, HD))

    def home(t):
        half, span = columns(t)
        return pltpu.make_async_remote_copy(
            src_ref=p_send.at[half, x, :, span], dst_ref=p_recv.at[half, y, :, span],
            send_sem=p_s.at[t, 3], recv_sem=p_r.at[t, y], device_id=feature_home, device_id_type=MESH,
        )

    def project(t):
        half, span = columns(t)
        for k in (1, 0, 2):
            send(p_send.at[half, x_at[k], :, span], p_recv.at[half, y, :, span], p_s.at[t, k], p_r.at[t, y], feature_peers[k])

        @pl.when(away)
        def _():
            home(t).start()

        @pl.when(jnp.logical_not(away))
        def _():
            p_recv[half, y, :, span] = p_send[half, x, :, span]

    def product(side, rows_of):
        pieces = [wt[side, lax.rem(v + QUAD - zq, QUAD)].reshape(NC * rows, width) for v in range(QUAD)]
        block = jnp.concatenate(pieces, axis=0)[rows_of]
        term = lax.dot_general(attended, block, NT, preferred_element_type=F32).astype(BF)
        return term.reshape(NX, rows, term.shape[1])

    def gather(t):
        half, span = columns(t)
        for k in range(3):
            arrive(p_recv.at[half, y_at[k], :, span], p_s.at[t, k], p_r.at[t, y_at[k]])

        @pl.when(away)
        def _():
            home(t).wait_recv()

        return jnp.sum(p_recv[half, :, :, span].astype(F32), axis=0)

    w_done(far)
    for t in range(heads):
        p_send[0, :, :, t * HD : (t + 1) * HD] = product(far, slice(t * HD, (t + 1) * HD))
        project(t)
    w_core(near)
    for t in range(heads):
        span = pl.ds(t * HD, HD)
        z_send[:, span] = gather(t).astype(BF)
        if t == 0:
            pl.semaphore_wait(entered, 1)
        send(z_send.at[:, span], z_recv.at[:, span], zz_s.at[t], zz_r.at[t], zh_peer)
    w_done(near)
    p_send[1] = product(near, slice(0, width))
    project(heads)
    rest = gather(heads) + bias_v[...].reshape(1, width)
    for t in range(heads):
        span = pl.ds(t * HD, HD)
        arrive(z_recv.at[:, span], zz_s.at[t], zz_r.at[t])
    out_ref[...] = (gate_v[...].reshape(1, width) * (rest + z_recv[...].astype(F32))).astype(BF)
    for cp in pending:
        cp.wait_send()

    @pl.when(away)
    def _():
        for t in range(heads + 1):
            home(t).wait_send()


def body(queries, stale_kv, codes, exponents, text_kv, out_weight, out_bias, out_gate):
    rows, width = queries.shape
    heads = width // HD
    dma = pltpu.SemaphoreType.DMA
    any_spec = pl.BlockSpec(memory_space=pl.ANY)
    return pl.pallas_call(
        kernel,
        out_shape=pltpu.VMEM((rows, width), BF),
        in_specs=[any_spec] * 8,
        out_specs=pl.BlockSpec(memory_space=pltpu.VMEM),
        scratch_shapes=[
            pltpu.VMEM(codes.shape, jnp.int32),
            pltpu.VMEM((heads, 2, rows), jnp.int32),
            pltpu.VMEM((width,), F32),
            pltpu.VMEM((width,), F32),
            pltpu.VMEM((2, NX, 2, NC * rows, width), BF),
            pltpu.VMEM((2, text_kv.shape[1] // QUAD, width), BF),
            pltpu.VMEM((QUAD, rows, width), BF),
            pltpu.VMEM((heads, 2, NX, 2, NC, rows, HD), BF),
            pltpu.VMEM((2, QUAD, NC, rows, width), BF),
            pltpu.VMEM((heads, QUAD, rows + STATS, HD), BF),
            pltpu.VMEM((heads, QUAD, rows + STATS, HD), BF),
            pltpu.VMEM((heads, NX, rows, HD), BF),
            pltpu.VMEM((2, NX, rows, width), BF),
            pltpu.VMEM((2, NY, rows, width), BF),
            pltpu.VMEM((rows, width), BF),
            pltpu.VMEM((rows, width), BF),
            dma((15,)),
            dma((3,)), dma((QUAD,)),
            dma((heads,)), dma((heads,)),
            dma((3,)), dma((NX,)),
            dma((heads, 3)), dma((heads, NX)),
            dma((heads + 1,)), dma((heads + 1,)),
            dma(()), dma(()),
            dma((2, 3)), dma((2, QUAD)),
            dma((2,)), dma((2,)),
            dma((heads, 3)), dma((heads, QUAD)),
            dma((heads, 3)), dma((heads, NX)),
            dma((heads + 1, 4)), dma((heads + 1, NY)),
            dma((heads,)), dma((heads,)),
            pltpu.SemaphoreType.REGULAR,
        ],
        compiler_params=pltpu.CompilerParams(
            collective_id=0, has_side_effects=True, vmem_limit_bytes=60 * 1024 * 1024
        ),
        cost_estimate=pl.CostEstimate(flops=640_000_000, bytes_accessed=4_000_000, transcendentals=520_000),
        name="joint_attention",
    )(
        queries, stale_kv, codes, exponents.transpose(2, 0, 1), text_kv, out_weight.T,
        out_bias, out_gate,
    )


def solution(mesh):
    placed = (
        P("patch", "head"),
        P(None, None, "head"),
        P(None, "patch", "head"),
        P(None, "patch", "head"),
        P(None, None, "head"),
        P("head", "patch"),
        P("head"),
        P("head"),
    )
    return jax.shard_map(
        body, mesh=mesh, in_specs=placed, out_specs=P("patch", "head"), check_vma=False
    )
```

```python
import jax
import jax.numpy as jnp
from jax import lax
from jax.experimental import pallas as pl
from jax.experimental.pallas import tpu as pltpu
from jax.sharding import PartitionSpec as P

HD = 128
NX, NZ, NC, NY, NH = 4, 8, 2, 4, 2
QUAD = 4
BF = jnp.bfloat16
F32 = jnp.float32
MESH = pl.DeviceIdType.MESH
NT = (((1,), (1,)), ((), ()))
NN = (((1,), (0,)), ((), ()))
TN = (((0,), (0,)), ((), ()))
STATS = 16


def kernel(
    q_hbm, stale_hbm, codes_hbm, exps_hbm, text_hbm, w_hbm, bias_hbm, gate_hbm,
    out_ref,
    codes_v, exps_v, bias_v, gate_v, stale_v, text_v,
    q_all, kv, wt, o_send, o_recv, a_all, p_send, p_recv, z_send, z_recv,
    lsem, q_s, q_r, kh_s, kh_r, kx_s, kx_r, kf_s, kf_r, kc_s, kc_r,
    wh_s, wh_r, wq_s, wq_r, wc_s, wc_r, o_s, o_r, a_s, a_r, p_s, p_r, zz_s, zz_r, entered,
):
    rows, width = q_hbm.shape
    heads = width // HD
    text_rows = text_hbm.shape[1] // QUAD
    p = lax.axis_index("patch")
    hd = lax.axis_index("head")
    x = lax.div(p, NZ * NC)
    z = lax.rem(lax.div(p, NC), NZ)
    c = lax.rem(p, NC)
    y = lax.div(hd, NH)
    zh = lax.rem(hd, NH)
    zb = lax.div(z, QUAD)
    zq = lax.rem(z, QUAD)
    far, near = 1 - zh, zh

    def dev(xx=x, z_=z, cc=c, yy=y, hh=zh):
        return (xx * (NZ * NC) + z_ * NC + cc, yy * NH + hh)

    def ring(k):
        at = lax.rem(zh * NZ + z + k, NZ * NH)
        return dev(z_=lax.rem(at, NZ), hh=lax.div(at, NZ))

    core_peer = dev(cc=1 - c)
    half_peer = dev(z_=(1 - zb) * QUAD + zq)
    zh_peer = dev(hh=1 - zh)
    x_at = [lax.rem(x + k, NX) for k in (1, 2, 3)]
    y_at = [lax.rem(y + k, NY) for k in (1, 2, 3)]
    q_at = [lax.rem(zq + k, QUAD) for k in (1, 2, 3)]
    x_peers = [dev(xx=v) for v in x_at]
    feature_peers = [dev(xx=v, yy=x) for v in x_at]
    feature_home = dev(yy=x)
    feature_from = [dev(xx=y, yy=v) for v in y_at]
    away = x != y
    feature_near = dev(xx=y, cc=jnp.where(away, c, 1 - c))
    q_peers = [dev(z_=zb * QUAD + v) for v in q_at]

    pending = []

    def send(src, dst, s, r, to):
        cp = pltpu.make_async_remote_copy(
            src_ref=src, dst_ref=dst, send_sem=s, recv_sem=r, device_id=to, device_id_type=MESH
        )
        cp.start()
        pending.append(cp)

    def arrive(dst, s, r):
        pltpu.make_async_remote_copy(
            src_ref=dst, dst_ref=dst, send_sem=s, recv_sem=r, device_id=core_peer, device_id_type=MESH
        ).wait_recv()

    barrier = pltpu.get_barrier_semaphore()
    everyone = [ring(4), ring(NZ * NH - 4), core_peer] + x_peers + q_peers
    for peer in everyone + feature_from + [feature_near]:
        pl.semaphore_signal(barrier, inc=1, device_id=peer, device_id_type=MESH)

    ld_codes = pltpu.make_async_copy(codes_hbm, codes_v, lsem.at[0])
    ld_exps = pltpu.make_async_copy(exps_hbm, exps_v, lsem.at[1])
    ld_w = pltpu.make_async_copy(w_hbm, wt.at[zb, 0, c], lsem.at[2])
    ld_q = pltpu.make_async_copy(q_hbm, q_all.at[zq], lsem.at[3])
    ld_text = pltpu.make_async_copy(text_hbm.at[:, pl.ds(zq * text_rows, text_rows)], text_v, lsem.at[4])
    ld_bias = pltpu.make_async_copy(bias_hbm, bias_v, lsem.at[5])
    ld_gate = pltpu.make_async_copy(gate_hbm, gate_v, lsem.at[6])
    ld_stale = [
        pltpu.make_async_copy(
            stale_hbm.at[:, pl.ds((xx * NZ + b * QUAD + zq) * NC * rows, NC * rows)],
            stale_v.at[:, xx, b], lsem.at[7 + xx * 2 + b],
        )
        for xx in range(NX) for b in range(2)
    ]
    for ld in [ld_codes, ld_exps, ld_w, ld_q, ld_text, ld_bias, ld_gate] + ld_stale:
        ld.start()

    diagonal = lax.broadcasted_iota(jnp.int32, (rows, rows), 0) == lax.broadcasted_iota(jnp.int32, (rows, rows), 1)
    ones = jnp.ones((rows, HD), BF)
    ld_codes.wait()
    ld_exps.wait()
    for h in range(heads):
        code = codes_v[:, :, h * HD : (h + 1) * HD]
        for kind in range(2):
            step = jnp.left_shift(jnp.int32(1), exps_v[h, kind : kind + 1] + 9).astype(F32) * (2.0**-9)
            spread = jnp.where(diagonal, step, 0.0).astype(BF)
            step = lax.dot_general(spread, ones, NN, preferred_element_type=F32)
            kv[h, kind, x, zb, c] = (code[kind].astype(F32) * step).astype(BF)
    ld_w.wait()
    ld_q.wait()

    pl.semaphore_wait(barrier, len(everyone) + 4)
    pl.semaphore_signal(entered, inc=1, device_id=ring(4), device_id_type=MESH)

    def kv_half(h):
        mine = kv.at[h, :, x, zb, c]
        send(mine, mine, kh_s.at[h], kh_r.at[h], half_peer)

    def kv_x():
        for k in (1, 0, 2):
            mine = kv.at[:, :, x, zb, c]
            send(mine, mine, kx_s.at[k], kx_r.at[x], x_peers[k])

    def q_quad():
        for k in range(3):
            send(q_all.at[zq], q_all.at[zq], q_s.at[k], q_r.at[zq], q_peers[k])

    own_w = wt.at[zb, 0, c]
    half_w = wt.at[1 - zb, 0, c]

    def w_half():
        send(own_w, own_w, wh_s, wh_r, half_peer)

    def w_got_half():
        arrive(half_w, wh_s, wh_r)

    def w_quad(side):
        for k in range(3):
            send(wt.at[side, 0, c], wt.at[side, 3 - k, c], wq_s.at[side, k], wq_r.at[side, 3 - k], q_peers[k])

    def w_core(side):
        for k in range(3):
            arrive(wt.at[side, k + 1, c], wq_s.at[side, k], wq_r.at[side, k + 1])
        mine = wt.at[side, :, c]
        send(mine, mine, wc_s.at[side], wc_r.at[side], core_peer)

    def w_done(side):
        arrive(wt.at[side, :, 1 - c], wc_s.at[side], wc_r.at[side])

    def kv_on(h):
        slot = kv.at[h, :, x, 1 - zb, c]
        arrive(slot, kh_s.at[h], kh_r.at[h])
        for k in (1, 0, 2):
            send(slot, slot, kf_s.at[h, k], kf_r.at[h, x], x_peers[k])

    def kv_core():
        for k in range(3):
            there = kv.at[:, :, x_at[k], zb, c]
            arrive(there, kx_s.at[k], kx_r.at[x_at[k]])
        all_x = kv.at[:, :, :, zb, c]
        send(all_x, all_x, kc_s.at[0], kc_r.at[0], core_peer)

    def kv_core_on(h):
        for k in range(3):
            slot = kv.at[h, :, x_at[k], 1 - zb, c]
            arrive(slot, kf_s.at[h, k], kf_r.at[h, x_at[k]])
        slot = kv.at[h, :, :, 1 - zb, c]
        send(slot, slot, kc_s.at[1 + h], kc_r.at[1 + h], core_peer)

    def ready():
        for k in range(3):
            arrive(q_all.at[q_at[k]], q_s.at[k], q_r.at[q_at[k]])
        for ld in [ld_text, ld_bias, ld_gate] + ld_stale:
            ld.wait()
        all_x = kv.at[:, :, :, zb, 1 - c]
        arrive(all_x, kc_s.at[0], kc_r.at[0])

    scale = HD**-0.5
    tokens = QUAD * rows
    keys = NX * 2 * NC * rows
    lane = lax.broadcasted_iota(jnp.int32, (tokens, HD), 1)
    first_row = lax.broadcasted_iota(jnp.int32, (STATS, HD), 0)
    first = (first_row == lax.broadcasted_iota(jnp.int32, (STATS, HD), 1)).astype(F32).astype(BF)

    def attend(h):
        slot = kv.at[h, :, :, 1 - zb, 1 - c]
        arrive(slot, kc_s.at[1 + h], kc_r.at[1 + h])
        cut = slice(h * HD, (h + 1) * HD)
        q = q_all[:, :, cut].reshape(tokens, HD)
        k_img = jnp.concatenate([stale_v[0, :, :, :, cut].reshape(keys, HD), kv[h, 0].reshape(keys, HD)], axis=1)
        v_img = jnp.concatenate([stale_v[1, :, :, :, cut].reshape(keys, HD), kv[h, 1].reshape(keys, HD)], axis=1)
        s_img = lax.dot_general(jnp.concatenate([q, q], axis=1), k_img, NT, preferred_element_type=F32)
        s_txt = lax.dot_general(q, text_v[0, :, cut], NT, preferred_element_type=F32)
        peak = jnp.maximum(jnp.max(s_img, axis=1, keepdims=True), jnp.max(s_txt, axis=1, keepdims=True))
        w_img = jnp.exp((s_img - peak) * scale).astype(BF)
        w_txt = jnp.exp((s_txt - peak) * scale).astype(BF)
        total = jnp.sum(w_img.astype(F32), axis=1, keepdims=True) + jnp.sum(w_txt.astype(F32), axis=1, keepdims=True)
        o_img = lax.dot_general(w_img, v_img, NN, preferred_element_type=F32)
        o_txt = lax.dot_general(w_txt, text_v[1, :, cut], NN, preferred_element_type=F32)
        o = (o_img[:, :HD] + o_img[:, HD:] + o_txt) / total
        stats = jnp.where(lane < 3, peak, total)
        third = lax.rem(lane, 3)
        top = stats.astype(BF).astype(F32)
        mid = (stats - top).astype(BF).astype(F32)
        low = stats - top - mid
        terms = jnp.where(third == 0, top, jnp.where(third == 1, mid, low))
        terms = terms.astype(BF)
        o_send[h, :, :rows] = o.astype(BF).reshape(QUAD, rows, HD)
        for v in range(QUAD):
            turned = lax.dot_general(first, terms[v * rows : (v + 1) * rows], NT, preferred_element_type=F32)
            o_send[h, v, rows:, :rows] = turned.astype(BF)
        for k in range(3):
            send(o_send.at[h, q_at[k]], o_recv.at[h, zq], o_s.at[h, k], o_r.at[h, zq], q_peers[k])

    pick_row = lax.broadcasted_iota(jnp.int32, (STATS, 2 * HD), 0)
    pick_col = lax.broadcasted_iota(jnp.int32, (STATS, 2 * HD), 1)
    pick = (lax.div(pick_row, 3) == lax.div(pick_col, HD)).astype(F32).astype(BF)

    def combine(h):
        o_recv[h, zq] = o_send[h, zq]
        for k in range(3):
            arrive(o_recv.at[h, q_at[k]], o_s.at[h, k], o_r.at[h, q_at[k]])
        wide = [
            lax.dot_general(o_recv[h, v, rows:, :rows], pick, TN, preferred_element_type=F32) for v in range(QUAD)
        ]
        peak = jnp.maximum(jnp.maximum(wide[0], wide[1]), jnp.maximum(wide[2], wide[3]))[:, :HD]
        shares = [jnp.exp((w[:, :HD] - peak) * scale) * w[:, HD:] for w in wide]
        mix = sum(shares[v] * o_recv[h, v, :rows].astype(F32) for v in range(QUAD)) / sum(shares)
        a_all[h, x] = mix.astype(BF)
        for k in (1, 0, 2):
            send(a_all.at[h, x], a_all.at[h, x], a_s.at[h, k], a_r.at[h, x], x_peers[k])

    kv_half(0)
    kv_x()
    kv_half(1)
    kv_half(2)
    q_quad()
    kv_core()
    kv_on(0)
    w_half()
    kv_on(1)
    kv_on(2)
    kv_core_on(0)
    w_got_half()
    w_quad(far)
    kv_core_on(1)
    ready()
    attend(0)
    kv_core_on(2)
    attend(1)
    attend(2)
    combine(0)
    w_core(far)
    combine(1)
    w_quad(near)
    combine(2)

    for h in range(heads):
        for k in range(3):
            arrive(a_all.at[h, x_at[k]], a_s.at[h, k], a_r.at[h, x_at[k]])
    attended = jnp.concatenate([a_all[h].reshape(NX * rows, HD) for h in range(heads)], axis=1)

    def columns(t):
        return (1, pl.ds(0, width)) if t == heads else (0, pl.ds(t * HD, HD))

    def home(t):
        half, span = columns(t)
        return pltpu.make_async_remote_copy(
            src_ref=p_send.at[half, x, :, span], dst_ref=p_recv.at[half, y, :, span],
            send_sem=p_s.at[t, 3], recv_sem=p_r.at[t, y], device_id=feature_home, device_id_type=MESH,
        )

    def project(t):
        half, span = columns(t)
        for k in (1, 0, 2):
            send(p_send.at[half, x_at[k], :, span], p_recv.at[half, y, :, span], p_s.at[t, k], p_r.at[t, y], feature_peers[k])

        @pl.when(away)
        def _():
            home(t).start()

        @pl.when(jnp.logical_not(away))
        def _():
            p_recv[half, y, :, span] = p_send[half, x, :, span]

    def product(side, rows_of):
        pieces = [wt[side, lax.rem(v + QUAD - zq, QUAD)].reshape(NC * rows, width) for v in range(QUAD)]
        block = jnp.concatenate(pieces, axis=0)[rows_of]
        term = lax.dot_general(attended, block, NT, preferred_element_type=F32).astype(BF)
        return term.reshape(NX, rows, term.shape[1])

    def gather(t):
        half, span = columns(t)
        for k in range(3):
            arrive(p_recv.at[half, y_at[k], :, span], p_s.at[t, k], p_r.at[t, y_at[k]])

        @pl.when(away)
        def _():
            home(t).wait_recv()

        return jnp.sum(p_recv[half, :, :, span].astype(F32), axis=0)

    w_done(far)
    for t in range(heads):
        p_send[0, :, :, t * HD : (t + 1) * HD] = product(far, slice(t * HD, (t + 1) * HD))
        project(t)
    w_core(near)
    for t in range(heads):
        span = pl.ds(t * HD, HD)
        z_send[:, span] = gather(t).astype(BF)
        if t == 0:
            pl.semaphore_wait(entered, 1)
        send(z_send.at[:, span], z_recv.at[:, span], zz_s.at[t], zz_r.at[t], zh_peer)
    w_done(near)
    p_send[1] = product(near, slice(0, width))
    project(heads)
    rest = gather(heads) + bias_v[...].reshape(1, width)
    for t in range(heads):
        span = pl.ds(t * HD, HD)
        arrive(z_recv.at[:, span], zz_s.at[t], zz_r.at[t])
    out_ref[...] = (gate_v[...].reshape(1, width) * (rest + z_recv[...].astype(F32))).astype(BF)
    for cp in pending:
        cp.wait_send()

    @pl.when(away)
    def _():
        for t in range(heads + 1):
            home(t).wait_send()


def body(queries, stale_kv, codes, exponents, text_kv, out_weight, out_bias, out_gate):
    rows, width = queries.shape
    heads = width // HD
    dma = pltpu.SemaphoreType.DMA
    any_spec = pl.BlockSpec(memory_space=pl.ANY)
    return pl.pallas_call(
        kernel,
        out_shape=pltpu.VMEM((rows, width), BF),
        in_specs=[any_spec] * 8,
        out_specs=pl.BlockSpec(memory_space=pltpu.VMEM),
        scratch_shapes=[
            pltpu.VMEM(codes.shape, jnp.int32),
            pltpu.VMEM((heads, 2, rows), jnp.int32),
            pltpu.VMEM((width,), F32),
            pltpu.VMEM((width,), F32),
            pltpu.VMEM((2, NX, 2, NC * rows, width), BF),
            pltpu.VMEM((2, text_kv.shape[1] // QUAD, width), BF),
            pltpu.VMEM((QUAD, rows, width), BF),
            pltpu.VMEM((heads, 2, NX, 2, NC, rows, HD), BF),
            pltpu.VMEM((2, QUAD, NC, rows, width), BF),
            pltpu.VMEM((heads, QUAD, rows + STATS, HD), BF),
            pltpu.VMEM((heads, QUAD, rows + STATS, HD), BF),
            pltpu.VMEM((heads, NX, rows, HD), BF),
            pltpu.VMEM((2, NX, rows, width), BF),
            pltpu.VMEM((2, NY, rows, width), BF),
            pltpu.VMEM((rows, width), BF),
            pltpu.VMEM((rows, width), BF),
            dma((15,)),
            dma((3,)), dma((QUAD,)),
            dma((heads,)), dma((heads,)),
            dma((3,)), dma((NX,)),
            dma((heads, 3)), dma((heads, NX)),
            dma((heads + 1,)), dma((heads + 1,)),
            dma(()), dma(()),
            dma((2, 3)), dma((2, QUAD)),
            dma((2,)), dma((2,)),
            dma((heads, 3)), dma((heads, QUAD)),
            dma((heads, 3)), dma((heads, NX)),
            dma((heads + 1, 4)), dma((heads + 1, NY)),
            dma((heads,)), dma((heads,)),
            pltpu.SemaphoreType.REGULAR,
        ],
        compiler_params=pltpu.CompilerParams(
            collective_id=0, has_side_effects=True, vmem_limit_bytes=60 * 1024 * 1024
        ),
        cost_estimate=pl.CostEstimate(flops=640_000_000, bytes_accessed=4_000_000, transcendentals=520_000),
        name="joint_attention",
    )(
        queries, stale_kv, codes, exponents.transpose(2, 0, 1), text_kv, out_weight.T,
        out_bias, out_gate,
    )


def solution(mesh):
    placed = (
        P("patch", "head"),
        P(None, None, "head"),
        P(None, "patch", "head"),
        P(None, "patch", "head"),
        P(None, None, "head"),
        P("head", "patch"),
        P("head"),
        P("head"),
    )
    return jax.shard_map(
        body, mesh=mesh, in_specs=placed, out_specs=P("patch", "head"), check_vma=False
    )
```
